512 devices in a mesh: edge: 128 (over z, y, core), mp: 4 (over x).
Axes of the slice: x: 4, y: 8, z: 8, core: 2. Of those that a mesh axis runs over, the one named last changes fastest.
Arguments:
- edge_feat: bfloat16 [262144, 512], P('edge', 'mp'), may hold values from -6 to 6
- mirror_rows: int32 [262144], P('edge'), may hold values from 0 to 2047, as said below
- edge_slot: int32 [2048, 128], P('edge'), may hold values from 0 to 15
- group_owner: int32 [8192, 1], P('edge'), may hold values from 0 to 127; in each aligned block of 64 rows (0 to 63, 64 to 127, ...) at most 2 rows name the same one
- group_window: int32 [8192], P('edge'), may hold values from 0 to 127
- up_edge: bfloat16 [512, 512], P(None, 'mp'), may hold values from -0.25 to 0.25
- down_edge: bfloat16 [512, 512], P('mp'), may hold values from -0.25 to 0.25
- mix_self: bfloat16 [512, 512], P(None, 'mp'), may hold values from -0.1875 to 0.1875
- mix_mirror: bfloat16 [512, 512], P(None, 'mp'), may hold values from -0.1875 to 0.1875
- up_atom: bfloat16 [512, 512], P(None, 'mp'), may hold values from -0.25 to 0.25
- down_atom: bfloat16 [512, 512], P('mp'), may hold values from -0.25 to 0.25
- atom_gain: float32 [512], replicated, may hold values from 0.1 to 1.9
Outputs:
- atom_out: bfloat16 [262144, 512], P('edge', 'mp')
The draws below stay inside these ranges and needn't reach their ends.
Inputs may be any that keep to these rules, and one draw needn't show every extreme that they name: Within each block of 2048 rows mirror_rows is a permutation; the partner block holds its inverse permutation, so the matching of reverse edges is symmetric. `group_owner`: among the 64 groups of one device, no owner is named more than 2 times, and in every draw some device names some owner exactly 2 times.
All inputs are finite; a program needn't handle non-finite values.
Results may differ from the reference program's by a relative error of at most 0.014.
Values may be sent and summed in bfloat16 or wider, within the bound.
No kernel may reach another device: no remote copies, remote signals or barrier semaphores. Data moves between devices by JAX's collectives and lax.ppermute only.
A program may use at most 64 MiB of HBM per device.

```python
import math
import jax
import jax.numpy as jnp
import numpy as np
from jax import lax

D = 512
H = 512
E_DEV = 2048
A_DEV = 2048
GR = 32
AW = 16
HB = 128
CAP = 2
EDGES = 262144
GROUPS = 8192
ATOMS = 262144
NW = 128
N_EDGE = 128


def draw_mirror_rows(key, part):
    blocks = EDGES // E_DEV
    half = blocks // 2
    keys = jax.random.split(jax.random.fold_in(key, 17), half)
    forward = jax.vmap(lambda k: jax.random.permutation(k, E_DEV))(keys).astype(jnp.int32)
    inverse = jnp.argsort(forward, axis=1, stable=True).astype(jnp.int32)
    return jnp.concatenate([forward, inverse], axis=0).reshape(EDGES).astype(jnp.int32)


def place_ends(array, key, least, largest):
    spot = [jax.random.randint(jax.random.fold_in(key, axis), (), 0, length) for axis, length in enumerate(array.shape)]
    longest = array.shape.index(max(array.shape))
    neighbour = spot[:longest] + [(spot[longest] + 1) % array.shape[longest]] + spot[longest + 1:]
    return array.at[tuple(spot)].set(least).at[tuple(neighbour)].set(largest)


def levels(stream_key, shape, shards, smallest, top_value):
    gain, own = 1.0, jax.random.fold_in(stream_key, 6)
    for axis_at, blocks in shards:
        heights = jnp.exp(jax.random.uniform(jax.random.fold_in(own, axis_at), (blocks,), jnp.float32, smallest / len(shards), top_value / len(shards)))
        gain = gain * jnp.repeat(heights, shape[axis_at] // blocks).reshape([-1 if axis == axis_at else 1 for axis in range(len(shape))])
    return gain


def routed_block(key, own, number, rows, amount, top, reach, slope):
    order = jax.random.permutation(key, amount)
    packed, common = portions_of(amount, rows * top, reach, slope, True), portions_of(amount, rows * top, reach, slope, False)
    places = jnp.arange(amount)

    def named(tallies, turn):
        used = int((tallies > 0).sum())
        fixed = max(1, used // 4)
        moved = fixed + (places - fixed + turn * (used - fixed)) % max(1, amount - fixed)
        return jnp.zeros((amount,), jnp.int32).at[order[jnp.where(places < fixed, places, moved)]].set(jnp.asarray(tallies, jnp.int32))

    tallies = jnp.where(number % 4 == 0, named(packed, number // 4), named(common, number - number // 4 - 1))
    mixed = jax.random.permutation(jax.random.fold_in(own, 3), amount)
    giver, taker = mixed[0:amount // 2 * 2:2], mixed[1:amount // 2 * 2:2]
    room = jnp.minimum(tallies[giver] - 1, reach - tallies[taker]) // 2
    room = jnp.where((giver == order[0]) | (taker == order[0]) | (tallies[taker] == 0), 0, jnp.maximum(room, 0))
    moved = jax.random.randint(jax.random.fold_in(own, 4), (amount // 2,), 0, 1 << 20) % (room + 1)
    tallies = tallies.at[giver].add(-moved).at[taker].add(moved)
    members = jnp.searchsorted(jnp.cumsum(tallies), jnp.arange(rows * top), side="right").astype(jnp.int32)
    grid = members.reshape(top, rows).T
    grid = grid[jax.random.permutation(jax.random.fold_in(own, 1), rows)]
    turn = jax.random.randint(jax.random.fold_in(own, 2), (rows, 1), 0, top)
    return jnp.take_along_axis(grid, (jnp.arange(top)[None, :] + turn) % top, axis=1)


def portions_of(count, total, most, skew, full):
    portions = [(1 << 20) // math.isqrt(standing ** skew) + 1 for standing in range(1, count + 1)]
    largest = most if full else min(most, max(-(-total // count), total * portions[0] // sum(portions)))
    least = 1 if total - largest >= count - 1 else 0
    given, surplus = [largest] + [least] * (count - 1), total - largest - least * (count - 1)
    while surplus > 0:
        candidates = [i for i in range(1, count) if given[i] < largest] or [i for i in range(1, count) if given[i] < most]
        pool, budget = sum([portions[i] for i in candidates]), surplus
        for i in candidates:
            more = min(most - given[i], max(1, budget * portions[i] // pool), surplus)
            given[i] = given[i] + more
            surplus = surplus - more
    return np.array(given)


def bell_draw(own_key, shape, deviation, limit, cuts=(), kind=jnp.bfloat16):
    result = jax.random.normal(own_key, shape, jnp.float32) * deviation
    if len(cuts) > 0:
        result = levels(own_key, shape, cuts, -0.22, 0.18) * result
    return jnp.clip(result, min=-limit, max=limit).astype(kind)


def setup_inputs(seed: int = 0) -> dict:
    streams_of = jax.random.split(jax.random.key(seed), 13)
    edge_feat = bell_draw(streams_of[0], (EDGES, D), 1.0, 6.0, ((0, 128), (1, 4)))
    mirror_rows = draw_mirror_rows(jax.random.fold_in(streams_of[12], 71), 0)
    edge_slot = place_ends(jax.random.randint(streams_of[2], (EDGES // 128, 128), 0, AW), jax.random.fold_in(streams_of[2], 1), 0, AW - 1).astype(jnp.int32)
    group_owner_keys = jax.random.split(jax.random.fold_in(streams_of[3], 1), GROUPS // (E_DEV // GR))
    group_owner_turns = jax.random.permutation(jax.random.fold_in(streams_of[3], 3), GROUPS // (E_DEV // GR))
    group_owner = jax.vmap(lambda own, number: routed_block(jax.random.fold_in(streams_of[3], 2), own, number, E_DEV // GR, N_EDGE, 1, CAP, 2))(group_owner_keys, group_owner_turns).reshape((GROUPS, 1))
    group_window = place_ends(jax.random.randint(streams_of[4], (GROUPS,), 0, NW), jax.random.fold_in(streams_of[4], 1), 0, NW - 1).astype(jnp.int32)
    up_edge = bell_draw(streams_of[5], (D, H), D ** -0.5, 0.25, ((1, 4),))
    down_edge = bell_draw(streams_of[6], (H, D), H ** -0.5, 0.25, ((0, 4),))
    mix_self = bell_draw(streams_of[7], (D, D), (2 * D) ** -0.5, 0.1875, ((1, 4),))
    mix_mirror = bell_draw(streams_of[8], (D, D), (2 * D) ** -0.5, 0.1875, ((1, 4),))
    up_atom = bell_draw(streams_of[9], (D, H), D ** -0.5, 0.25, ((1, 4),))
    down_atom = bell_draw(streams_of[10], (H, D), H ** -0.5, 0.25, ((0, 4),))
    atom_gain = jnp.clip(1.0 + 0.18 * jax.random.normal(streams_of[11], (D,), jnp.float32), 0.1, 1.9)
    return dict(edge_feat=edge_feat, mirror_rows=mirror_rows, edge_slot=edge_slot, group_owner=group_owner, group_window=group_window, up_edge=up_edge, down_edge=down_edge, mix_self=mix_self, mix_mirror=mix_mirror, up_atom=up_atom, down_atom=down_atom, atom_gain=atom_gain)


def blocked_down(hidden, down):
    total = jnp.zeros((hidden.shape[0], down.shape[1]), jnp.float32)
    for k in range(H // HB):
        part = jnp.dot(hidden[:, k * HB:(k + 1) * HB], down[k * HB:(k + 1) * HB], preferred_element_type=jnp.float32)
        total = total + part.astype(jnp.bfloat16).astype(jnp.float32)
    return total

def reference(edge_feat, mirror_rows, edge_slot, group_owner, group_window, up_edge, down_edge, mix_self, mix_mirror, up_atom, down_atom, atom_gain):
    edge_pre = jnp.dot(edge_feat, up_edge, preferred_element_type=jnp.float32)
    edge_hidden = jax.nn.silu(edge_pre).astype(jnp.bfloat16)
    edge_one = (edge_feat.astype(jnp.float32) + blocked_down(edge_hidden, down_edge)).astype(jnp.bfloat16)
    blocks = EDGES // E_DEV
    stacked = edge_one.reshape(blocks, E_DEV, D)
    partner = jnp.bitwise_xor(jnp.arange(blocks, dtype=jnp.int32), blocks // 2)
    mirrored = stacked[partner]
    picks = mirror_rows.reshape(blocks, E_DEV)[:, :, None].astype(jnp.int32)
    reverse = jnp.take_along_axis(mirrored, picks, axis=1).reshape(EDGES, D)
    mixed = jnp.dot(edge_one, mix_self, preferred_element_type=jnp.float32) + jnp.dot(reverse, mix_mirror, preferred_element_type=jnp.float32)
    edge_two = (edge_one.astype(jnp.float32) + jax.nn.silu(mixed)).astype(jnp.bfloat16)
    owner = jnp.repeat(group_owner[:, 0], GR)
    window = jnp.repeat(group_window, GR)
    target = (owner * A_DEV + window * AW + edge_slot.reshape(EDGES)).astype(jnp.int32)
    atom_sum = jax.ops.segment_sum(edge_two.astype(jnp.float32), target, num_segments=ATOMS).astype(jnp.bfloat16)
    atom_f = atom_sum.astype(jnp.float32)
    scale = lax.rsqrt(lax.optimization_barrier(jnp.mean(atom_f * atom_f, axis=1, keepdims=True)) + 1e-06)
    normed = (atom_f * scale * atom_gain.astype(jnp.float32)).astype(jnp.bfloat16)
    atom_hidden = jax.nn.silu(jnp.dot(normed, up_atom, preferred_element_type=jnp.float32)).astype(jnp.bfloat16)
    return (atom_f + blocked_down(atom_hidden, down_atom)).astype(jnp.bfloat16)
```

```python
import jax
import jax.numpy as jnp
from jax import lax
from jax.experimental import pallas as pl
from jax.experimental.pallas import tpu as pltpu
from jax.sharding import PartitionSpec as P

A_DEV = 2048
GR = 32
AW = 16
MP = 4
F = 128
D = 512
ROWS = 2048
OWN = ROWS // MP
GROUPS = ROWS // GR
OWNERS = 128
CAP = 2
VMEM = pltpu.VMEM
LIMIT = 48 * 1024 * 1024


def silu(v):
    return v / (1.0 + jnp.exp(-v))


def vmem_spec():
    return pl.BlockSpec(memory_space=pltpu.VMEM)


def smem_spec():
    return pl.BlockSpec(memory_space=pltpu.SMEM)


def params():
    return pltpu.CompilerParams(vmem_limit_bytes=LIMIT)


def mm(a, b):
    return jnp.dot(a, b, preferred_element_type=jnp.float32)


def gather_kernel(rows_ref, mirror_ref, out_ref):
    step = 256
    lanes = lax.broadcasted_iota(jnp.int32, (step, F), 1)

    @pl.loop(0, ROWS // step)
    def _(k):
        picks = []
        for half in range(step // F):
            line = mirror_ref[pl.ds(k * (step // F) + half, 1), :]
            picks.append(jnp.broadcast_to(line, (F, F)).T)
        pick = jnp.concatenate(picks, axis=0)
        hot = jnp.concatenate(
            [
                jnp.where(pick == lanes + j * F, 1.0, 0.0).astype(jnp.bfloat16)
                for j in range(ROWS // F)
            ],
            axis=1,
        )
        got = mm(hot, rows_ref[...])
        out_ref[pl.ds(pl.multiple_of(k * step, step), step), :] = got.astype(jnp.bfloat16)


def gather_rows(rows, mirror):
    return pl.pallas_call(
        gather_kernel,
        out_shape=jax.ShapeDtypeStruct((ROWS, F), jnp.bfloat16),
        in_specs=[vmem_spec()] * 2,
        out_specs=vmem_spec(),
        compiler_params=params(),
        name="gather_rows",
    )(rows, mirror.reshape(ROWS // F, F))


def windows_kernel(owner_ref, window_ref, out_ref):
    owner = owner_ref[...]
    hot = lax.broadcasted_iota(jnp.int32, (OWNERS, GROUPS), 0) == owner
    before = lax.broadcasted_iota(jnp.int32, (GROUPS, GROUPS), 0) < lax.broadcasted_iota(
        jnp.int32, (GROUPS, GROUPS), 1
    )
    rank = mm(
        jnp.where(hot, 1.0, 0.0).astype(jnp.bfloat16),
        jnp.where(before, 1.0, 0.0).astype(jnp.bfloat16),
    )
    value = window_ref[...].astype(jnp.float32) + 1.0
    lane = lax.broadcasted_iota(jnp.int32, (OWNERS, F), 1)
    out = jnp.full((OWNERS, F), -1.0, jnp.float32)
    for r in range(CAP):
        mine = jnp.where(hot & (rank == float(r)), value, 0.0)
        out = jnp.where(lane == r, jnp.sum(mine, axis=1, keepdims=True) - 1.0, out)
    out_ref[...] = out.astype(jnp.bfloat16)


def send_windows(owner, window):
    return pl.pallas_call(
        windows_kernel,
        out_shape=jax.ShapeDtypeStruct((OWNERS, F), jnp.bfloat16),
        in_specs=[vmem_spec()] * 2,
        out_specs=vmem_spec(),
        compiler_params=params(),
        name="send_windows",
    )(owner.reshape(1, GROUPS), window.reshape(1, GROUPS))


def wide(ref, start, pair):
    return jnp.concatenate(
        [ref[2 * pair, start : start + D, :], ref[2 * pair + 1, start : start + D, :]], axis=1
    )


def down_wide(ref, start, pair):
    blocks = [
        jnp.concatenate([ref[m, start + j * F : start + (j + 1) * F, :] for j in (2 * pair, 2 * pair + 1)], axis=1)
        for m in range(MP)
    ]
    return jnp.concatenate(blocks, axis=0)


def side_by_side(ref):
    return jnp.concatenate([ref[m] for m in range(MP)], axis=1)


def mlp(inputs, base, w_ref, up_at, down_at):
    hidden = jnp.concatenate(
        [silu(mm(inputs, wide(w_ref, up_at, p))).astype(jnp.bfloat16) for p in range(2)], axis=1
    )
    return [
        (base[:, 2 * F * p : 2 * F * (p + 1)].astype(jnp.float32) + mm(hidden, down_wide(w_ref, down_at, p))).astype(
            jnp.bfloat16
        )
        for p in range(2)
    ]


def edge_kernel(own_ref, rev_ref, slot_ref, w_ref, out_ref):
    own = side_by_side(own_ref)
    rev = side_by_side(rev_ref)
    one = jnp.concatenate(mlp(own, own, w_ref, 0, D), axis=1)
    reverse = jnp.concatenate(mlp(rev, rev, w_ref, 0, D), axis=1)
    groups = OWN // GR
    at = lax.broadcasted_iota(jnp.int32, (groups * AW, OWN), 0)
    target = slot_ref[...] + (lax.broadcasted_iota(jnp.int32, (1, OWN), 1) // GR) * AW
    pick = jnp.where(at == target, 1.0, 0.0).astype(jnp.bfloat16)
    for p in range(2):
        mixed = mm(one, wide(w_ref, 2 * D, p)) + mm(reverse, wide(w_ref, 3 * D, p))
        two = (one[:, 2 * F * p : 2 * F * (p + 1)].astype(jnp.float32) + silu(mixed)).astype(jnp.bfloat16)
        sums = mm(pick, two).astype(jnp.bfloat16)
        out_ref[2 * p] = sums[:, :F]
        out_ref[2 * p + 1] = sums[:, F:]


def edge_stage(own, rev, slots, weights):
    return pl.pallas_call(
        edge_kernel,
        out_shape=jax.ShapeDtypeStruct((MP, OWN // GR * AW, F), jnp.bfloat16),
        in_specs=[vmem_spec()] * 4,
        out_specs=vmem_spec(),
        compiler_params=params(),
        name="edge_stage",
    )(own, rev, slots, weights)


def place_kernel(owner_ref, blocks_ref, out_ref, seen_ref):
    @pl.loop(0, OWNERS, unroll=8)
    def _(o):
        seen_ref[o] = 0

    out_ref[...] = jnp.zeros_like(out_ref)

    @pl.loop(0, GROUPS, unroll=4)
    def _(g):
        owner = owner_ref[g]
        rank = seen_ref[owner]
        seen_ref[owner] = rank + 1
        out_ref[owner * CAP + rank] = blocks_ref[g]


def place(owner, blocks):
    return pl.pallas_call(
        place_kernel,
        out_shape=jax.ShapeDtypeStruct((OWNERS * CAP, AW, F), jnp.bfloat16),
        in_specs=[smem_spec(), vmem_spec()],
        out_specs=vmem_spec(),
        scratch_shapes=[pltpu.SMEM((OWNERS,), jnp.int32)],
        compiler_params=params(),
        name="place_groups",
    )(owner, blocks)


def atom_kernel(x_ref, gain_ref, w_ref, out_ref):
    base = side_by_side(x_ref)
    full = base.astype(jnp.float32)
    scale = lax.rsqrt(jnp.mean(full * full, axis=1, keepdims=True) + 1e-06)
    normed = (full * scale * gain_ref[...]).astype(jnp.bfloat16)
    out = mlp(normed, base, w_ref, 0, D)
    for p in range(2):
        out_ref[2 * p] = out[p][:, :F]
        out_ref[2 * p + 1] = out[p][:, F:]


def atom_stage(x, gain, weights):
    return pl.pallas_call(
        atom_kernel,
        out_shape=jax.ShapeDtypeStruct((MP, OWN, F), jnp.bfloat16),
        in_specs=[vmem_spec()] * 3,
        out_specs=vmem_spec(),
        compiler_params=params(),
        name="atom_stage",
    )(x, gain.reshape(1, D), weights)


def transpose_mp(x):
    return lax.all_to_all(x, "mp", split_axis=0, concat_axis=0, tiled=True)


def columns(down):
    return [down[:, j * F : (j + 1) * F] for j in range(MP)]


def body(
    edge_feat,
    mirror_rows,
    edge_slot,
    group_owner,
    group_window,
    up_edge,
    down_edge,
    mix_self,
    mix_mirror,
    up_atom,
    down_atom,
    atom_gain,
):
    half = OWNERS // 2
    partner = lax.ppermute(edge_feat, "edge", [(e, e ^ half) for e in range(OWNERS)])
    edge_w = lax.all_gather(
        jnp.concatenate([up_edge, *columns(down_edge), mix_self, mix_mirror], axis=0), "mp", axis=0
    )
    atom_w = lax.all_gather(jnp.concatenate([up_atom, *columns(down_atom)], axis=0), "mp", axis=0)
    owner = group_owner.reshape(GROUPS)
    got_windows = lax.all_to_all(
        send_windows(owner, group_window).reshape(OWNERS, 1, F), "edge", split_axis=0, concat_axis=0, tiled=True
    )
    own = transpose_mp(edge_feat.reshape(MP, OWN, F))
    rev = transpose_mp(gather_rows(partner, mirror_rows).reshape(MP, OWN, F))
    me = lax.axis_index("mp")
    slots = lax.dynamic_slice(edge_slot, (me * (OWN // F), 0), (OWN // F, F)).reshape(1, OWN)
    partial = edge_stage(own, rev, slots, edge_w)
    blocks = transpose_mp(partial).reshape(GROUPS, AW, F)
    got = lax.all_to_all(place(owner, blocks), "edge", split_axis=0, concat_axis=0, tiled=True)
    win = got_windows[:, 0, :CAP].reshape(1, OWNERS * CAP).astype(jnp.float32)
    windows = A_DEV // AW
    placing = (win == jnp.arange(windows, dtype=jnp.float32)[:, None]).astype(jnp.bfloat16)
    atom_sum = jnp.dot(
        placing, got.reshape(OWNERS * CAP, AW * F), preferred_element_type=jnp.float32
    ).astype(jnp.bfloat16)
    x = transpose_mp(atom_sum.reshape(MP, OWN, F))
    return transpose_mp(atom_stage(x, atom_gain, atom_w)).reshape(A_DEV, F)


def solution(mesh):
    in_specs = (
        P("edge", "mp"),
        P("edge"),
        P("edge", None),
        P("edge", None),
        P("edge"),
        P(None, "mp"),
        P("mp", None),
        P(None, "mp"),
        P(None, "mp"),
        P(None, "mp"),
        P("mp", None),
        P(),
    )
    out_specs = P("edge", "mp")
    return jax.shard_map(body, mesh=mesh, in_specs=in_specs, out_specs=out_specs, check_vma=False)
```

```python
import jax
import jax.numpy as jnp
from jax import lax
from jax.experimental import pallas as pl
from jax.experimental.pallas import tpu as pltpu
from jax.sharding import PartitionSpec as P

A_DEV = 2048
GR = 32
AW = 16
MP = 4
F = 128
D = 512
ROWS = 2048
OWN = ROWS // MP
GROUPS = ROWS // GR
OWNERS = 128
CAP = 2
HEAD = 8
VMEM = pltpu.VMEM
LIMIT = 48 * 1024 * 1024
ALL_VMEM = 63 * 1024 * 1024


def silu(v):
    return v / (1.0 + jnp.exp(-v))


def vmem_spec():
    return pl.BlockSpec(memory_space=pltpu.VMEM)


def smem_spec():
    return pl.BlockSpec(memory_space=pltpu.SMEM)


def params():
    return pltpu.CompilerParams(vmem_limit_bytes=LIMIT)


def mm(a, b):
    return jnp.dot(a, b, preferred_element_type=jnp.float32)


def gather_kernel(rows_ref, mirror_ref, out_ref):
    step = 1024
    lanes = lax.broadcasted_iota(jnp.int32, (step, F), 1)

    @pl.loop(0, ROWS // step)
    def _(k):
        picks = []
        for half in range(step // F):
            line = mirror_ref[pl.ds(k * (step // F) + half, 1), :]
            picks.append(jnp.broadcast_to(line, (F, F)).T)
        pick = jnp.concatenate(picks, axis=0)
        hot = jnp.concatenate(
            [
                jnp.where(pick == lanes + j * F, 1.0, 0.0).astype(jnp.bfloat16)
                for j in range(ROWS // F)
            ],
            axis=1,
        )
        got = mm(hot, rows_ref[...])
        out_ref[pl.ds(pl.multiple_of(k * step, step), step), :] = got.astype(jnp.bfloat16)


def gather_rows(rows, mirror):
    return pl.pallas_call(
        gather_kernel,
        out_shape=jax.ShapeDtypeStruct((ROWS, F), jnp.bfloat16),
        in_specs=[vmem_spec()] * 2,
        out_specs=vmem_spec(),
        compiler_params=params(),
        name="gather_rows",
    )(rows, mirror.reshape(ROWS // F, F))


def windows_kernel(owner_ref, window_ref, out_ref):
    owner = owner_ref[...]
    hot = lax.broadcasted_iota(jnp.int32, (OWNERS, GROUPS), 0) == owner
    before = lax.broadcasted_iota(jnp.int32, (GROUPS, GROUPS), 0) < lax.broadcasted_iota(
        jnp.int32, (GROUPS, GROUPS), 1
    )
    rank = mm(
        jnp.where(hot, 1.0, 0.0).astype(jnp.bfloat16),
        jnp.where(before, 1.0, 0.0).astype(jnp.bfloat16),
    )
    value = window_ref[...].astype(jnp.float32) + 1.0
    lane = lax.broadcasted_iota(jnp.int32, (OWNERS, F), 1)
    out = jnp.full((OWNERS, F), -1.0, jnp.float32)
    for r in range(CAP):
        mine = jnp.where(hot & (rank == float(r)), value, 0.0)
        out = jnp.where(lane == r, jnp.sum(mine, axis=1, keepdims=True) - 1.0, out)
    out_ref[...] = out.astype(jnp.bfloat16)


def send_windows(owner, window):
    return pl.pallas_call(
        windows_kernel,
        out_shape=jax.ShapeDtypeStruct((OWNERS, F), jnp.bfloat16),
        in_specs=[vmem_spec()] * 2,
        out_specs=vmem_spec(),
        compiler_params=params(),
        name="send_windows",
    )(owner.reshape(1, GROUPS), window.reshape(1, GROUPS))


def pack_kernel(*refs):
    *sources, out_ref, held, sems = refs
    copies = []
    for k, source in enumerate(sources):
        if source.shape[0] == D:
            moves = [(source, held.at[pl.ds(k * D, D)])]
        else:
            moves = [
                (source.at[:, pl.ds(j * F, F)], held.at[pl.ds(k * D + j * F, F)]) for j in range(MP)
            ]
        for source_part, part in moves:
            copies.append(pltpu.make_async_copy(source_part, part, sems.at[len(copies)]))
    for copy in copies:
        copy.start()
    for copy in copies:
        copy.wait()
    whole = pltpu.make_async_copy(held, out_ref, sems.at[len(copies)])
    whole.start()
    whole.wait()


def pack(*weights, limit):
    rows = len(weights) * D
    return pl.pallas_call(
        pack_kernel,
        out_shape=jax.ShapeDtypeStruct((rows, F), jnp.bfloat16),
        in_specs=[pl.BlockSpec(memory_space=pl.ANY)] * len(weights),
        out_specs=pl.BlockSpec(memory_space=pl.ANY),
        scratch_shapes=[pltpu.VMEM((rows, F), jnp.bfloat16), pltpu.SemaphoreType.DMA((len(weights) * MP + 1,))],
        compiler_params=pltpu.CompilerParams(vmem_limit_bytes=limit),
        name="pack_weights",
    )(*weights)


def wide(ref, start, pair):
    return jnp.concatenate(
        [ref[2 * pair, start : start + D, :], ref[2 * pair + 1, start : start + D, :]], axis=1
    )


def down_wide(ref, start, pair):
    blocks = [
        jnp.concatenate([ref[m, start + j * F : start + (j + 1) * F, :] for j in (2 * pair, 2 * pair + 1)], axis=1)
        for m in range(MP)
    ]
    return jnp.concatenate(blocks, axis=0)


def side_by_side(ref):
    return jnp.concatenate([ref[m] for m in range(MP)], axis=1)


def mlp(inputs, base, w_ref, up_at, down_at):
    hidden = jnp.concatenate(
        [silu(mm(inputs, wide(w_ref, up_at, p))).astype(jnp.bfloat16) for p in range(2)], axis=1
    )
    return [
        (base[:, 2 * F * p : 2 * F * (p + 1)].astype(jnp.float32) + mm(hidden, down_wide(w_ref, down_at, p))).astype(
            jnp.bfloat16
        )
        for p in range(2)
    ]


def edge_kernel(own_ref, rev_ref, slot_ref, w_ref, out_ref):
    own = side_by_side(own_ref)
    rev = side_by_side(rev_ref)
    one = jnp.concatenate(mlp(own, own, w_ref, 0, D), axis=1)
    reverse = jnp.concatenate(mlp(rev, rev, w_ref, 0, D), axis=1)
    groups = OWN // GR
    at = lax.broadcasted_iota(jnp.int32, (groups * AW, OWN), 0)
    target = slot_ref[...] + (lax.broadcasted_iota(jnp.int32, (1, OWN), 1) // GR) * AW
    pick = jnp.where(at == target, 1.0, 0.0).astype(jnp.bfloat16)
    for p in range(2):
        mixed = mm(one, wide(w_ref, 2 * D, p)) + mm(reverse, wide(w_ref, 3 * D, p))
        two = (one[:, 2 * F * p : 2 * F * (p + 1)].astype(jnp.float32) + silu(mixed)).astype(jnp.bfloat16)
        sums = mm(pick, two).astype(jnp.bfloat16)
        out_ref[2 * p] = sums[:, :F]
        out_ref[2 * p + 1] = sums[:, F:]


def edge_stage(own, rev, slots, weights):
    return pl.pallas_call(
        edge_kernel,
        out_shape=jax.ShapeDtypeStruct((MP, OWN // GR * AW, F), jnp.bfloat16),
        in_specs=[vmem_spec()] * 4,
        out_specs=vmem_spec(),
        compiler_params=params(),
        name="edge_stage",
    )(own, rev, slots, weights)


def place_kernel(owner_ref, window_ref, blocks_ref, out_ref, seen_ref):
    @pl.loop(0, OWNERS, unroll=8)
    def _(o):
        seen_ref[o] = 0

    out_ref[:, : CAP * AW, :] = jnp.zeros((OWNERS, CAP * AW, F), jnp.bfloat16)
    out_ref[:, CAP * AW :, :] = jnp.full((OWNERS, HEAD, F), -1.0, jnp.bfloat16)
    line = lax.broadcasted_iota(jnp.int32, (HEAD, F), 0)

    @pl.loop(0, GROUPS, unroll=4)
    def _(g):
        owner = owner_ref[g]
        rank = seen_ref[owner]
        seen_ref[owner] = rank + 1
        out_ref[owner, pl.ds(pl.multiple_of(rank * AW, AW), AW), :] = blocks_ref[g]
        head = out_ref[owner, CAP * AW :, :].astype(jnp.float32)
        head = jnp.where(line == rank, window_ref[g].astype(jnp.float32), head)
        out_ref[owner, CAP * AW :, :] = head.astype(jnp.bfloat16)


def place(owner, window, blocks):
    return pl.pallas_call(
        place_kernel,
        out_shape=jax.ShapeDtypeStruct((OWNERS, CAP * AW + HEAD, F), jnp.bfloat16),
        in_specs=[smem_spec(), smem_spec(), vmem_spec()],
        out_specs=vmem_spec(),
        scratch_shapes=[pltpu.SMEM((OWNERS,), jnp.int32)],
        compiler_params=params(),
        name="place_groups",
    )(owner, window, blocks)


def collect_kernel(got_ref, out_ref, wide_ref, sum_ref):
    period = CAP * AW + HEAD
    wide_ref[...] = got_ref[...].astype(jnp.float32).reshape(OWNERS * period, F)
    lanes = lax.broadcasted_iota(jnp.int32, (OWNERS, F), 1).astype(jnp.float32)
    placing = jnp.concatenate(
        [
            jnp.where(wide_ref[pl.ds(CAP * AW + r, OWNERS, stride=period), :] == lanes, 1.0, 0.0).T
            for r in range(CAP)
        ],
        axis=1,
    ).astype(jnp.bfloat16)
    for a in range(0, AW, 2):
        rows = jnp.concatenate(
            [
                jnp.concatenate(
                    [wide_ref[pl.ds(r * AW + b, OWNERS, stride=period), :] for b in (a, a + 1)], axis=1
                )
                for r in range(CAP)
            ],
            axis=0,
        ).astype(jnp.bfloat16)
        sums = mm(placing, rows)
        sum_ref[pl.ds(a, A_DEV // AW, stride=AW), :] = sums[:, :F]
        sum_ref[pl.ds(a + 1, A_DEV // AW, stride=AW), :] = sums[:, F:]
    out_ref[...] = sum_ref[...].astype(jnp.bfloat16).reshape(MP, OWN, F)


def collect(got):
    return pl.pallas_call(
        collect_kernel,
        out_shape=jax.ShapeDtypeStruct((MP, OWN, F), jnp.bfloat16),
        in_specs=[vmem_spec()],
        out_specs=vmem_spec(),
        scratch_shapes=[
            pltpu.VMEM((OWNERS * (CAP * AW + HEAD), F), jnp.float32),
            pltpu.VMEM((A_DEV, F), jnp.float32),
        ],
        compiler_params=params(),
        name="collect_blocks",
    )(got)


def atom_kernel(x_ref, gain_ref, w_ref, out_ref):
    base = side_by_side(x_ref)
    full = base.astype(jnp.float32)
    scale = lax.rsqrt(jnp.mean(full * full, axis=1, keepdims=True) + 1e-06)
    normed = (full * scale * gain_ref[...]).astype(jnp.bfloat16)
    out = mlp(normed, base, w_ref, 0, D)
    for p in range(2):
        out_ref[2 * p] = out[p][:, :F]
        out_ref[2 * p + 1] = out[p][:, F:]


def atom_stage(x, gain, weights):
    return pl.pallas_call(
        atom_kernel,
        out_shape=jax.ShapeDtypeStruct((MP, OWN, F), jnp.bfloat16),
        in_specs=[vmem_spec()] * 3,
        out_specs=vmem_spec(),
        compiler_params=params(),
        name="atom_stage",
    )(x, gain.reshape(1, D), weights)


def transpose_mp(x):
    return lax.all_to_all(x, "mp", split_axis=0, concat_axis=0, tiled=True)


def body(
    edge_feat,
    mirror_rows,
    edge_slot,
    group_owner,
    group_window,
    up_edge,
    down_edge,
    mix_self,
    mix_mirror,
    up_atom,
    down_atom,
    atom_gain,
):
    half = OWNERS // 2
    partner = lax.ppermute(edge_feat, "edge", [(e, e ^ half) for e in range(OWNERS)])
    edge_w = lax.all_gather(
        pack(up_edge, down_edge, mix_self, mix_mirror, limit=ALL_VMEM), "mp", axis=0
    )
    owner = group_owner.reshape(GROUPS)
    own = transpose_mp(edge_feat.reshape(MP, OWN, F))
    rev = transpose_mp(gather_rows(partner, mirror_rows).reshape(MP, OWN, F))
    me = lax.axis_index("mp")
    slots = lax.dynamic_slice(edge_slot, (me * (OWN // F), 0), (OWN // F, F)).reshape(1, OWN)
    partial = edge_stage(own, rev, slots, edge_w)
    partial, up_atom, down_atom = lax.optimization_barrier((partial, up_atom, down_atom))
    atom_w = lax.all_gather(pack(up_atom, down_atom, limit=LIMIT), "mp", axis=0)
    blocks = transpose_mp(partial).reshape(GROUPS, AW, F)
    sent = place(owner, group_window, blocks)
    got = lax.all_to_all(sent, "edge", split_axis=0, concat_axis=0, tiled=True)
    x = transpose_mp(collect(got))
    return transpose_mp(atom_stage(x, atom_gain, atom_w)).reshape(A_DEV, F)


def solution(mesh):
    in_specs = (
        P("edge", "mp"),
        P("edge"),
        P("edge", None),
        P("edge", None),
        P("edge"),
        P(None, "mp"),
        P("mp", None),
        P(None, "mp"),
        P(None, "mp"),
        P(None, "mp"),
        P("mp", None),
        P(),
    )
    out_specs = P("edge", "mp")
    return jax.shard_map(body, mesh=mesh, in_specs=in_specs, out_specs=out_specs, check_vma=False)
```

```python
import jax
import jax.numpy as jnp
from jax import lax
from jax.experimental import pallas as pl
from jax.experimental.pallas import tpu as pltpu
from jax.sharding import PartitionSpec as P

A_DEV = 2048
GR = 32
AW = 16
MP = 4
F = 128
D = 512
ROWS = 2048
OWN = ROWS // MP
PIECE = OWN + 2 * D
GROUPS = ROWS // GR
OWNERS = 128
CAP = 2
HEAD = 8
VMEM = pltpu.VMEM
LIMIT = 24 * 1024 * 1024
ALL_VMEM = 63 * 1024 * 1024


def silu(v):
    return v / (1.0 + jnp.exp(-v))


def vmem_spec():
    return pl.BlockSpec(memory_space=pltpu.VMEM)


def smem_spec():
    return pl.BlockSpec(memory_space=pltpu.SMEM)


def params():
    return pltpu.CompilerParams(vmem_limit_bytes=LIMIT)


def mm(a, b):
    return jnp.dot(a, b, preferred_element_type=jnp.float32)


def gather_kernel(rows_ref, mirror_ref, out_ref):
    step = 1024
    lanes = lax.broadcasted_iota(jnp.int32, (step, F), 1)

    @pl.loop(0, ROWS // step)
    def _(k):
        picks = []
        for half in range(step // F):
            line = mirror_ref[pl.ds(k * (step // F) + half, 1), :]
            picks.append(jnp.broadcast_to(line, (F, F)).T)
        pick = jnp.concatenate(picks, axis=0)
        hot = jnp.concatenate(
            [
                jnp.where(pick == lanes + j * F, 1.0, 0.0).astype(jnp.bfloat16)
                for j in range(ROWS // F)
            ],
            axis=1,
        )
        got = mm(hot, rows_ref[...])
        out_ref[pl.ds(pl.multiple_of(k * step, step), step), :] = got.astype(jnp.bfloat16)


def gather_rows(rows, mirror):
    return pl.pallas_call(
        gather_kernel,
        out_shape=jax.ShapeDtypeStruct((ROWS, F), jnp.bfloat16),
        in_specs=[vmem_spec()] * 2,
        out_specs=vmem_spec(),
        compiler_params=params(),
        cost_estimate=pl.CostEstimate(flops=20_000_000_000, bytes_accessed=64_000_000, transcendentals=0),
        name="gather_rows",
    )(rows, mirror.reshape(ROWS // F, F))


def windows_kernel(owner_ref, window_ref, out_ref):
    owner = owner_ref[...]
    hot = lax.broadcasted_iota(jnp.int32, (OWNERS, GROUPS), 0) == owner
    before = lax.broadcasted_iota(jnp.int32, (GROUPS, GROUPS), 0) < lax.broadcasted_iota(
        jnp.int32, (GROUPS, GROUPS), 1
    )
    rank = mm(
        jnp.where(hot, 1.0, 0.0).astype(jnp.bfloat16),
        jnp.where(before, 1.0, 0.0).astype(jnp.bfloat16),
    )
    value = window_ref[...].astype(jnp.float32) + 1.0
    lane = lax.broadcasted_iota(jnp.int32, (OWNERS, F), 1)
    out = jnp.full((OWNERS, F), -1.0, jnp.float32)
    for r in range(CAP):
        mine = jnp.where(hot & (rank == float(r)), value, 0.0)
        out = jnp.where(lane == r, jnp.sum(mine, axis=1, keepdims=True) - 1.0, out)
    out_ref[...] = out.astype(jnp.bfloat16)


def send_windows(owner, window):
    return pl.pallas_call(
        windows_kernel,
        out_shape=jax.ShapeDtypeStruct((OWNERS, F), jnp.bfloat16),
        in_specs=[vmem_spec()] * 2,
        out_specs=vmem_spec(),
        compiler_params=params(),
        name="send_windows",
    )(owner.reshape(1, GROUPS), window.reshape(1, GROUPS))


def pack_kernel(*refs):
    *sources, out_ref, held, sems = refs
    copies = []
    for k, source in enumerate(sources):
        if source.shape[0] == D:
            moves = [(source, held.at[pl.ds(k * D, D)])]
        else:
            moves = [
                (source.at[:, pl.ds(j * F, F)], held.at[pl.ds(k * D + j * F, F)]) for j in range(MP)
            ]
        for source_part, part in moves:
            copies.append(pltpu.make_async_copy(source_part, part, sems.at[len(copies)]))
    for copy in copies:
        copy.start()
    for copy in copies:
        copy.wait()
    whole = pltpu.make_async_copy(held, out_ref, sems.at[len(copies)])
    whole.start()
    whole.wait()


def pack(*weights, limit):
    rows = len(weights) * D
    return pl.pallas_call(
        pack_kernel,
        out_shape=jax.ShapeDtypeStruct((rows, F), jnp.bfloat16),
        in_specs=[pl.BlockSpec(memory_space=pl.ANY)] * len(weights),
        out_specs=pl.BlockSpec(memory_space=pl.ANY),
        scratch_shapes=[pltpu.VMEM((rows, F), jnp.bfloat16), pltpu.SemaphoreType.DMA((len(weights) * MP + 1,))],
        compiler_params=pltpu.CompilerParams(vmem_limit_bytes=limit),
        name="pack_weights",
    )(*weights)


def core_index():
    return lax.rem(lax.axis_index("edge"), 2)


def share_kernel(rows_ref, up_ref, down_ref, self_ref, mirror_ref, out_ref, held, sems):
    def move(moves):
        copies = [pltpu.make_async_copy(src, dst, sems.at[k]) for k, (src, dst) in enumerate(moves)]
        for copy in copies:
            copy.start()
        for copy in copies:
            copy.wait()

    own = [(rows_ref, held.at[:, pl.ds(0, OWN)])]
    core = core_index()

    @pl.when(core == 0)
    def _():
        moves = list(own)
        for m in range(MP):
            moves.append((up_ref, held.at[m, pl.ds(OWN, D)]))
            for j in range(MP):
                moves.append((down_ref.at[:, pl.ds(j * F, F)], held.at[m, pl.ds(OWN + D + j * F, F)]))
        move(moves)

    @pl.when(core != 0)
    def _():
        moves = list(own)
        for m in range(MP):
            moves.append((self_ref, held.at[m, pl.ds(OWN, D)]))
            moves.append((mirror_ref, held.at[m, pl.ds(OWN + D, D)]))
        move(moves)

    move([(held, out_ref)])


def share(rows, *weights):
    return pl.pallas_call(
        share_kernel,
        out_shape=jax.ShapeDtypeStruct((MP, PIECE, F), jnp.bfloat16),
        in_specs=[pl.BlockSpec(memory_space=pl.ANY)] * 5,
        out_specs=pl.BlockSpec(memory_space=pl.ANY),
        scratch_shapes=[
            pltpu.VMEM((MP, PIECE, F), jnp.bfloat16),
            pltpu.SemaphoreType.DMA((1 + MP * (1 + MP),)),
        ],
        compiler_params=pltpu.CompilerParams(vmem_limit_bytes=ALL_VMEM),
        name="share_rows_and_weights",
    )(rows, *weights)


def wide(ref, start, pair):
    return jnp.concatenate(
        [ref[2 * pair, start : start + D, :], ref[2 * pair + 1, start : start + D, :]], axis=1
    )


def down_wide(ref, start, pair):
    blocks = [
        jnp.concatenate([ref[m, start + j * F : start + (j + 1) * F, :] for j in (2 * pair, 2 * pair + 1)], axis=1)
        for m in range(MP)
    ]
    return jnp.concatenate(blocks, axis=0)


def side_by_side(ref):
    return jnp.concatenate([ref[m] for m in range(MP)], axis=1)


def up(inputs, w_ref, at):
    return jnp.concatenate(
        [silu(mm(inputs, wide(w_ref, at, p))).astype(jnp.bfloat16) for p in range(2)], axis=1
    )


def down(hidden, base, w_ref, at):
    return [
        (base[:, 2 * F * p : 2 * F * (p + 1)].astype(jnp.float32) + mm(hidden, down_wide(w_ref, at, p))).astype(
            jnp.bfloat16
        )
        for p in range(2)
    ]


def edge_kernel(mine_ref, other_hbm, rev_ref, slot_ref, out_ref, other_ref, sems):
    copies = [
        pltpu.make_async_copy(
            other_hbm.at[:, pl.ds(OWN + k * D, D)], other_ref.at[:, pl.ds(OWN + k * D, D)], sems.at[k]
        )
        for k in range(2)
    ]
    for copy in copies:
        copy.start()

    def run(mlp_ref, mix_ref):
        own = jnp.concatenate([mine_ref[m, :OWN] for m in range(MP)], axis=1)
        rev = side_by_side(rev_ref)
        if mlp_ref is other_ref:
            copies[0].wait()
        own_hidden = up(own, mlp_ref, OWN)
        rev_hidden = up(rev, mlp_ref, OWN)
        if mlp_ref is other_ref:
            copies[1].wait()
        one = jnp.concatenate(down(own_hidden, own, mlp_ref, OWN + D), axis=1)
        reverse = jnp.concatenate(down(rev_hidden, rev, mlp_ref, OWN + D), axis=1)
        if mix_ref is other_ref:
            copies[0].wait()
            copies[1].wait()
        groups = OWN // GR
        at = lax.broadcasted_iota(jnp.int32, (groups * AW, OWN), 0)
        target = slot_ref[...] + (lax.broadcasted_iota(jnp.int32, (1, OWN), 1) // GR) * AW
        pick = jnp.where(at == target, 1.0, 0.0).astype(jnp.bfloat16)
        for p in range(2):
            mixed = mm(one, wide(mix_ref, OWN, p)) + mm(reverse, wide(mix_ref, OWN + D, p))
            two = (one[:, 2 * F * p : 2 * F * (p + 1)].astype(jnp.float32) + silu(mixed)).astype(jnp.bfloat16)
            sums = mm(pick, two).astype(jnp.bfloat16)
            out_ref[2 * p] = sums[:, :F]
            out_ref[2 * p + 1] = sums[:, F:]

    core = core_index()

    @pl.when(core == 0)
    def _():
        run(mine_ref, other_ref)

    @pl.when(core != 0)
    def _():
        run(other_ref, mine_ref)


def edge_stage(mine, other, rev, slots):
    return pl.pallas_call(
        edge_kernel,
        out_shape=jax.ShapeDtypeStruct((MP, OWN // GR * AW, F), jnp.bfloat16),
        in_specs=[vmem_spec(), pl.BlockSpec(memory_space=pl.ANY), vmem_spec(), vmem_spec()],
        out_specs=vmem_spec(),
        scratch_shapes=[pltpu.VMEM((MP, PIECE, F), jnp.bfloat16), pltpu.SemaphoreType.DMA((2,))],
        compiler_params=params(),
        name="edge_stage",
    )(mine, other, rev, slots)


def place_kernel(owner_ref, window_ref, blocks_ref, out_ref, seen_ref):
    @pl.loop(0, OWNERS, unroll=8)
    def _(o):
        seen_ref[o] = 0

    out_ref[:, : CAP * AW, :] = jnp.zeros((OWNERS, CAP * AW, F), jnp.bfloat16)
    out_ref[:, CAP * AW :, :] = jnp.full((OWNERS, HEAD, F), -1.0, jnp.bfloat16)
    line = lax.broadcasted_iota(jnp.int32, (HEAD, F), 0)

    @pl.loop(0, GROUPS, unroll=4)
    def _(g):
        owner = owner_ref[g]
        rank = seen_ref[owner]
        seen_ref[owner] = rank + 1
        out_ref[owner, pl.ds(pl.multiple_of(rank * AW, AW), AW), :] = blocks_ref[g]
        head = out_ref[owner, CAP * AW :, :].astype(jnp.float32)
        head = jnp.where(line == rank, window_ref[g].astype(jnp.float32), head)
        out_ref[owner, CAP * AW :, :] = head.astype(jnp.bfloat16)


def place(owner, window, blocks):
    return pl.pallas_call(
        place_kernel,
        out_shape=jax.ShapeDtypeStruct((OWNERS, CAP * AW + HEAD, F), jnp.bfloat16),
        in_specs=[smem_spec(), smem_spec(), vmem_spec()],
        out_specs=vmem_spec(),
        scratch_shapes=[pltpu.SMEM((OWNERS,), jnp.int32)],
        compiler_params=params(),
        name="place_groups",
    )(owner, window, blocks)


def collect_kernel(got_ref, out_ref, wide_ref, sum_ref):
    period = CAP * AW + HEAD
    wide_ref[...] = got_ref[...].astype(jnp.float32).reshape(OWNERS * period, F)
    lanes = lax.broadcasted_iota(jnp.int32, (OWNERS, F), 1).astype(jnp.float32)
    placing = jnp.concatenate(
        [
            jnp.where(wide_ref[pl.ds(CAP * AW + r, OWNERS, stride=period), :] == lanes, 1.0, 0.0).T
            for r in range(CAP)
        ],
        axis=1,
    ).astype(jnp.bfloat16)
    for a in range(0, AW, 2):
        rows = jnp.concatenate(
            [
                jnp.concatenate(
                    [wide_ref[pl.ds(r * AW + b, OWNERS, stride=period), :] for b in (a, a + 1)], axis=1
                )
                for r in range(CAP)
            ],
            axis=0,
        ).astype(jnp.bfloat16)
        sums = mm(placing, rows)
        sum_ref[pl.ds(a, A_DEV // AW, stride=AW), :] = sums[:, :F]
        sum_ref[pl.ds(a + 1, A_DEV // AW, stride=AW), :] = sums[:, F:]
    out_ref[...] = sum_ref[...].astype(jnp.bfloat16).reshape(MP, OWN, F)


def collect(got):
    return pl.pallas_call(
        collect_kernel,
        out_shape=jax.ShapeDtypeStruct((MP, OWN, F), jnp.bfloat16),
        in_specs=[vmem_spec()],
        out_specs=vmem_spec(),
        scratch_shapes=[
            pltpu.VMEM((OWNERS * (CAP * AW + HEAD), F), jnp.float32),
            pltpu.VMEM((A_DEV, F), jnp.float32),
        ],
        compiler_params=params(),
        name="collect_blocks",
    )(got)


def atom_kernel(x_ref, gain_ref, *refs):
    *shards, out_ref, w_ref = refs
    me = lax.axis_index("mp")
    for shift, shard in enumerate(shards):
        w_ref[lax.rem(me + MP - shift, MP)] = shard[...]
    base = side_by_side(x_ref)
    full = base.astype(jnp.float32)
    scale = lax.rsqrt(jnp.mean(full * full, axis=1, keepdims=True) + 1e-06)
    normed = (full * scale * gain_ref[...]).astype(jnp.bfloat16)
    out = down(up(normed, w_ref, 0), base, w_ref, D)
    for p in range(2):
        out_ref[2 * p] = out[p][:, :F]
        out_ref[2 * p + 1] = out[p][:, F:]


def atom_stage(x, gain, shards):
    return pl.pallas_call(
        atom_kernel,
        out_shape=jax.ShapeDtypeStruct((MP, OWN, F), jnp.bfloat16),
        in_specs=[vmem_spec()] * (2 + MP),
        out_specs=vmem_spec(),
        scratch_shapes=[pltpu.VMEM((MP, 2 * D, F), jnp.bfloat16)],
        compiler_params=params(),
        name="atom_stage",
    )(x, gain.reshape(1, D), *shards)


def transpose_mp(x):
    return lax.all_to_all(x, "mp", split_axis=0, concat_axis=0, tiled=True)


def body(
    edge_feat,
    mirror_rows,
    edge_slot,
    group_owner,
    group_window,
    up_edge,
    down_edge,
    mix_self,
    mix_mirror,
    up_atom,
    down_atom,
    atom_gain,
):
    half = OWNERS // 2
    partner = lax.ppermute(edge_feat, "edge", [(e, e ^ half) for e in range(OWNERS)])
    owner = group_owner.reshape(GROUPS)
    mine = transpose_mp(
        share(edge_feat.reshape(MP, OWN, F), up_edge, down_edge, mix_self, mix_mirror)
    )
    reverse, mine = lax.optimization_barrier((gather_rows(partner, mirror_rows), mine))
    other = lax.ppermute(mine, "edge", [(e, e ^ 1) for e in range(OWNERS)])
    rev = transpose_mp(reverse.reshape(MP, OWN, F))
    me = lax.axis_index("mp")
    slots = lax.dynamic_slice(edge_slot, (me * (OWN // F), 0), (OWN // F, F)).reshape(1, OWN)
    partial = edge_stage(mine, other, rev, slots)
    blocks = transpose_mp(partial).reshape(GROUPS, AW, F)
    sent = place(owner, group_window, blocks)
    sent, up_atom, down_atom = lax.optimization_barrier((sent, up_atom, down_atom))
    atom_pack = pack(up_atom, down_atom, limit=LIMIT)
    atom_w = [atom_pack] + [
        lax.ppermute(atom_pack, "mp", [(m, (m + shift) % MP) for m in range(MP)]) for shift in range(1, MP)
    ]
    got = lax.all_to_all(sent, "edge", split_axis=0, concat_axis=0, tiled=True)
    got, *atom_w = lax.optimization_barrier((got, *atom_w))
    x = transpose_mp(collect(got))
    return transpose_mp(atom_stage(x, atom_gain, atom_w)).reshape(A_DEV, F)


def solution(mesh):
    in_specs = (
        P("edge", "mp"),
        P("edge"),
        P("edge", None),
        P("edge", None),
        P("edge"),
        P(None, "mp"),
        P("mp", None),
        P(None, "mp"),
        P(None, "mp"),
        P(None, "mp"),
        P("mp", None),
        P(),
    )
    out_specs = P("edge", "mp")
    return jax.shard_map(body, mesh=mesh, in_specs=in_specs, out_specs=out_specs, check_vma=False)
```

```python
import jax
import jax.numpy as jnp
from jax import lax
from jax.experimental import pallas as pl
from jax.experimental.pallas import tpu as pltpu
from jax.sharding import PartitionSpec as P

A_DEV = 2048
GR = 32
AW = 16
MP = 4
F = 128
D = 512
ROWS = 2048
OWN = ROWS // MP
PIECE = OWN + 2 * D
GROUPS = ROWS // GR
OWNERS = 128
CAP = 2
HEAD = 8
VMEM = pltpu.VMEM
LIMIT = 24 * 1024 * 1024
ALL_VMEM = 63 * 1024 * 1024


def silu(v):
    return 0.5 * v * (1.0 + jnp.tanh(0.5 * v))


def vmem_spec():
    return pl.BlockSpec(memory_space=pltpu.VMEM)


def smem_spec():
    return pl.BlockSpec(memory_space=pltpu.SMEM)


def params():
    return pltpu.CompilerParams(vmem_limit_bytes=LIMIT)


def mm(a, b):
    return jnp.dot(a, b, preferred_element_type=jnp.float32)


def gather_kernel(rows_ref, mirror_ref, out_ref):
    half = ROWS // 2
    pick = jnp.concatenate(
        [jnp.broadcast_to(mirror_ref[j : j + 1, :], (F, F)).T for j in range(ROWS // F)], axis=0
    )
    within = pick & (half - 1)
    lanes = lax.broadcasted_iota(jnp.int32, (ROWS, F), 1)
    hot = jnp.concatenate(
        [jnp.where(within == lanes + j * F, 1.0, 0.0).astype(jnp.bfloat16) for j in range(half // F)], axis=1
    )
    got = mm(hot, jnp.concatenate([rows_ref[:half], rows_ref[half:]], axis=1))
    out_ref[...] = jnp.where(pick >= half, got[:, F:], got[:, :F]).astype(jnp.bfloat16)


def gather_rows(rows, mirror):
    return pl.pallas_call(
        gather_kernel,
        out_shape=jax.ShapeDtypeStruct((ROWS, F), jnp.bfloat16),
        in_specs=[vmem_spec()] * 2,
        out_specs=vmem_spec(),
        compiler_params=params(),
        cost_estimate=pl.CostEstimate(flops=20_000_000_000, bytes_accessed=64_000_000, transcendentals=0),
        name="gather_rows",
    )(rows, mirror.reshape(ROWS // F, F))


def windows_kernel(owner_ref, window_ref, out_ref):
    owner = owner_ref[...]
    hot = lax.broadcasted_iota(jnp.int32, (OWNERS, GROUPS), 0) == owner
    before = lax.broadcasted_iota(jnp.int32, (GROUPS, GROUPS), 0) < lax.broadcasted_iota(
        jnp.int32, (GROUPS, GROUPS), 1
    )
    rank = mm(
        jnp.where(hot, 1.0, 0.0).astype(jnp.bfloat16),
        jnp.where(before, 1.0, 0.0).astype(jnp.bfloat16),
    )
    value = window_ref[...].astype(jnp.float32) + 1.0
    lane = lax.broadcasted_iota(jnp.int32, (OWNERS, F), 1)
    out = jnp.full((OWNERS, F), -1.0, jnp.float32)
    for r in range(CAP):
        mine = jnp.where(hot & (rank == float(r)), value, 0.0)
        out = jnp.where(lane == r, jnp.sum(mine, axis=1, keepdims=True) - 1.0, out)
    out_ref[...] = out.astype(jnp.bfloat16)


def send_windows(owner, window):
    return pl.pallas_call(
        windows_kernel,
        out_shape=jax.ShapeDtypeStruct((OWNERS, F), jnp.bfloat16),
        in_specs=[vmem_spec()] * 2,
        out_specs=vmem_spec(),
        compiler_params=params(),
        name="send_windows",
    )(owner.reshape(1, GROUPS), window.reshape(1, GROUPS))


def pack_kernel(*refs):
    *sources, out_ref, held, sems = refs
    copies = []
    for k, source in enumerate(sources):
        if source.shape[0] == D:
            moves = [(source, held.at[pl.ds(k * D, D)])]
        else:
            moves = [
                (source.at[:, pl.ds(j * F, F)], held.at[pl.ds(k * D + j * F, F)]) for j in range(MP)
            ]
        for source_part, part in moves:
            copies.append(pltpu.make_async_copy(source_part, part, sems.at[len(copies)]))
    for copy in copies:
        copy.start()
    for copy in copies:
        copy.wait()
    whole = pltpu.make_async_copy(held, out_ref, sems.at[len(copies)])
    whole.start()
    whole.wait()


def pack(*weights, limit):
    rows = len(weights) * D
    return pl.pallas_call(
        pack_kernel,
        out_shape=jax.ShapeDtypeStruct((rows, F), jnp.bfloat16),
        in_specs=[pl.BlockSpec(memory_space=pl.ANY)] * len(weights),
        out_specs=pl.BlockSpec(memory_space=pl.ANY),
        scratch_shapes=[pltpu.VMEM((rows, F), jnp.bfloat16), pltpu.SemaphoreType.DMA((len(weights) * MP + 1,))],
        compiler_params=pltpu.CompilerParams(vmem_limit_bytes=limit),
        name="pack_weights",
    )(*weights)


def core_index():
    return lax.rem(lax.axis_index("edge"), 2)


def share_kernel(rows_ref, up_ref, down_ref, self_ref, mirror_ref, out_ref, held, sems):
    def move(moves):
        copies = [pltpu.make_async_copy(src, dst, sems.at[k]) for k, (src, dst) in enumerate(moves)]
        for copy in copies:
            copy.start()
        for copy in copies:
            copy.wait()

    own = [(rows_ref, held.at[:, pl.ds(0, OWN)])]
    core = core_index()

    @pl.when(core == 0)
    def _():
        moves = list(own)
        for m in range(MP):
            moves.append((up_ref, held.at[m, pl.ds(OWN, D)]))
            for j in range(MP):
                moves.append((down_ref.at[:, pl.ds(j * F, F)], held.at[m, pl.ds(OWN + D + j * F, F)]))
        move(moves)

    @pl.when(core != 0)
    def _():
        moves = list(own)
        for m in range(MP):
            moves.append((self_ref, held.at[m, pl.ds(OWN, D)]))
            moves.append((mirror_ref, held.at[m, pl.ds(OWN + D, D)]))
        move(moves)

    move([(held, out_ref)])


def share(rows, *weights):
    return pl.pallas_call(
        share_kernel,
        out_shape=jax.ShapeDtypeStruct((MP, PIECE, F), jnp.bfloat16),
        in_specs=[pl.BlockSpec(memory_space=pl.ANY)] * 5,
        out_specs=pl.BlockSpec(memory_space=pl.ANY),
        scratch_shapes=[
            pltpu.VMEM((MP, PIECE, F), jnp.bfloat16),
            pltpu.SemaphoreType.DMA((1 + MP * (1 + MP),)),
        ],
        compiler_params=pltpu.CompilerParams(vmem_limit_bytes=ALL_VMEM),
        name="share_rows_and_weights",
    )(rows, *weights)


def wide(ref, start, pair):
    return jnp.concatenate(
        [ref[2 * pair, start : start + D, :], ref[2 * pair + 1, start : start + D, :]], axis=1
    )


def down_wide(ref, start, pair):
    blocks = [
        jnp.concatenate([ref[m, start + j * F : start + (j + 1) * F, :] for j in (2 * pair, 2 * pair + 1)], axis=1)
        for m in range(MP)
    ]
    return jnp.concatenate(blocks, axis=0)


def side_by_side(ref):
    return jnp.concatenate([ref[m] for m in range(MP)], axis=1)


def up(inputs, w_ref, at):
    return jnp.concatenate(
        [silu(mm(inputs, wide(w_ref, at, p))).astype(jnp.bfloat16) for p in range(2)], axis=1
    )


def down(hidden, base, w_ref, at):
    return [
        (base[:, 2 * F * p : 2 * F * (p + 1)].astype(jnp.float32) + mm(hidden, down_wide(w_ref, at, p))).astype(
            jnp.bfloat16
        )
        for p in range(2)
    ]


def edge_kernel(mine_ref, other_hbm, rev_ref, slot_ref, out_ref, other_ref, sems):
    copies = [
        pltpu.make_async_copy(
            other_hbm.at[:, pl.ds(OWN + k * D, D)], other_ref.at[:, pl.ds(OWN + k * D, D)], sems.at[k]
        )
        for k in range(2)
    ]
    for copy in copies:
        copy.start()

    def run(mlp_ref, mix_ref):
        own = jnp.concatenate([mine_ref[m, :OWN] for m in range(MP)], axis=1)
        rev = side_by_side(rev_ref)
        if mlp_ref is other_ref:
            copies[0].wait()
        own_hidden = up(own, mlp_ref, OWN)
        rev_hidden = up(rev, mlp_ref, OWN)
        if mlp_ref is other_ref:
            copies[1].wait()
        one = jnp.concatenate(down(own_hidden, own, mlp_ref, OWN + D), axis=1)
        reverse = jnp.concatenate(down(rev_hidden, rev, mlp_ref, OWN + D), axis=1)
        if mix_ref is other_ref:
            copies[0].wait()
            copies[1].wait()
        groups = OWN // GR
        at = lax.broadcasted_iota(jnp.int32, (groups * AW, OWN), 0)
        target = slot_ref[...] + (lax.broadcasted_iota(jnp.int32, (1, OWN), 1) // GR) * AW
        pick = jnp.where(at == target, 1.0, 0.0).astype(jnp.bfloat16)
        for p in range(2):
            mixed = mm(one, wide(mix_ref, OWN, p)) + mm(reverse, wide(mix_ref, OWN + D, p))
            two = (one[:, 2 * F * p : 2 * F * (p + 1)].astype(jnp.float32) + silu(mixed)).astype(jnp.bfloat16)
            sums = mm(pick, two).astype(jnp.bfloat16)
            out_ref[2 * p] = sums[:, :F]
            out_ref[2 * p + 1] = sums[:, F:]

    core = core_index()

    @pl.when(core == 0)
    def _():
        run(mine_ref, other_ref)

    @pl.when(core != 0)
    def _():
        run(other_ref, mine_ref)


def edge_stage(mine, other, rev, slots):
    return pl.pallas_call(
        edge_kernel,
        out_shape=jax.ShapeDtypeStruct((MP, OWN // GR * AW, F), jnp.bfloat16),
        in_specs=[vmem_spec(), pl.BlockSpec(memory_space=pl.ANY), vmem_spec(), vmem_spec()],
        out_specs=vmem_spec(),
        scratch_shapes=[pltpu.VMEM((MP, PIECE, F), jnp.bfloat16), pltpu.SemaphoreType.DMA((2,))],
        compiler_params=params(),
        name="edge_stage",
    )(mine, other, rev, slots)


def place_kernel(owner_ref, window_ref, blocks_ref, out_ref, seen_ref):
    @pl.loop(0, OWNERS, unroll=8)
    def _(o):
        seen_ref[o] = 0

    out_ref[:, : CAP * AW, :] = jnp.zeros((OWNERS, CAP * AW, F), jnp.bfloat16)
    out_ref[:, CAP * AW :, :] = jnp.full((OWNERS, HEAD, F), -1.0, jnp.bfloat16)
    line = lax.broadcasted_iota(jnp.int32, (HEAD, F), 0)

    @pl.loop(0, GROUPS, unroll=16)
    def _(g):
        owner = owner_ref[g]
        rank = seen_ref[owner]
        seen_ref[owner] = rank + 1
        out_ref[owner, pl.ds(pl.multiple_of(rank * AW, AW), AW), :] = blocks_ref[g]
        head = out_ref[owner, CAP * AW :, :].astype(jnp.float32)
        head = jnp.where(line == rank, window_ref[g].astype(jnp.float32), head)
        out_ref[owner, CAP * AW :, :] = head.astype(jnp.bfloat16)


def place(owner, window, blocks):
    return pl.pallas_call(
        place_kernel,
        out_shape=jax.ShapeDtypeStruct((OWNERS, CAP * AW + HEAD, F), jnp.bfloat16),
        in_specs=[smem_spec(), smem_spec(), vmem_spec()],
        out_specs=vmem_spec(),
        scratch_shapes=[pltpu.SMEM((OWNERS,), jnp.int32)],
        compiler_params=params(),
        name="place_groups",
    )(owner, window, blocks)


def collect_kernel(got_ref, out_ref, wide_ref, sum_ref):
    period = CAP * AW + HEAD
    wide_ref[...] = got_ref[...].astype(jnp.float32).reshape(OWNERS * period, F)
    lanes = lax.broadcasted_iota(jnp.int32, (OWNERS, F), 1).astype(jnp.float32)
    placing = jnp.concatenate(
        [
            jnp.where(wide_ref[pl.ds(CAP * AW + r, OWNERS, stride=period), :] == lanes, 1.0, 0.0).T
            for r in range(CAP)
        ],
        axis=1,
    ).astype(jnp.bfloat16)
    for a in range(0, AW, 2):
        rows = jnp.concatenate(
            [
                jnp.concatenate(
                    [wide_ref[pl.ds(r * AW + b, OWNERS, stride=period), :] for b in (a, a + 1)], axis=1
                )
                for r in range(CAP)
            ],
            axis=0,
        ).astype(jnp.bfloat16)
        sums = mm(placing, rows)
        sum_ref[pl.ds(a, A_DEV // AW, stride=AW), :] = sums[:, :F]
        sum_ref[pl.ds(a + 1, A_DEV // AW, stride=AW), :] = sums[:, F:]
    out_ref[...] = sum_ref[...].astype(jnp.bfloat16).reshape(MP, OWN, F)


def collect(got):
    return pl.pallas_call(
        collect_kernel,
        out_shape=jax.ShapeDtypeStruct((MP, OWN, F), jnp.bfloat16),
        in_specs=[vmem_spec()],
        out_specs=vmem_spec(),
        scratch_shapes=[
            pltpu.VMEM((OWNERS * (CAP * AW + HEAD), F), jnp.float32),
            pltpu.VMEM((A_DEV, F), jnp.float32),
        ],
        compiler_params=params(),
        name="collect_blocks",
    )(got)


def atom_kernel(x_ref, gain_ref, *refs):
    *shards, out_ref, w_ref = refs
    me = lax.axis_index("mp")
    for shift, shard in enumerate(shards):
        w_ref[lax.rem(me + MP - shift, MP)] = shard[...]
    base = side_by_side(x_ref)
    full = base.astype(jnp.float32)
    scale = lax.rsqrt(jnp.mean(full * full, axis=1, keepdims=True) + 1e-06)
    normed = (full * scale * gain_ref[...]).astype(jnp.bfloat16)
    out = down(up(normed, w_ref, 0), base, w_ref, D)
    for p in range(2):
        out_ref[2 * p] = out[p][:, :F]
        out_ref[2 * p + 1] = out[p][:, F:]


def atom_stage(x, gain, shards):
    return pl.pallas_call(
        atom_kernel,
        out_shape=jax.ShapeDtypeStruct((MP, OWN, F), jnp.bfloat16),
        in_specs=[vmem_spec()] * (2 + MP),
        out_specs=vmem_spec(),
        scratch_shapes=[pltpu.VMEM((MP, 2 * D, F), jnp.bfloat16)],
        compiler_params=params(),
        name="atom_stage",
    )(x, gain.reshape(1, D), *shards)


def transpose_mp(x):
    return lax.all_to_all(x, "mp", split_axis=0, concat_axis=0, tiled=True)


def body(
    edge_feat,
    mirror_rows,
    edge_slot,
    group_owner,
    group_window,
    up_edge,
    down_edge,
    mix_self,
    mix_mirror,
    up_atom,
    down_atom,
    atom_gain,
):
    half = OWNERS // 2
    partner = lax.ppermute(edge_feat, "edge", [(e, e ^ half) for e in range(OWNERS)])
    owner = group_owner.reshape(GROUPS)
    mine = transpose_mp(
        share(edge_feat.reshape(MP, OWN, F), up_edge, down_edge, mix_self, mix_mirror)
    )
    reverse, mine = lax.optimization_barrier((gather_rows(partner, mirror_rows), mine))
    other = lax.ppermute(mine, "edge", [(e, e ^ 1) for e in range(OWNERS)])
    rev = transpose_mp(reverse.reshape(MP, OWN, F))
    me = lax.axis_index("mp")
    slots = lax.dynamic_slice(edge_slot, (me * (OWN // F), 0), (OWN // F, F)).reshape(1, OWN)
    partial = edge_stage(mine, other, rev, slots)
    blocks = transpose_mp(partial).reshape(GROUPS, AW, F)
    sent = place(owner, group_window, blocks)
    sent, up_atom, down_atom = lax.optimization_barrier((sent, up_atom, down_atom))
    atom_pack = pack(up_atom, down_atom, limit=LIMIT)
    atom_w = [atom_pack] + [
        lax.ppermute(atom_pack, "mp", [(m, (m + shift) % MP) for m in range(MP)]) for shift in range(1, MP)
    ]
    got = lax.all_to_all(sent, "edge", split_axis=0, concat_axis=0, tiled=True)
    got, *atom_w = lax.optimization_barrier((got, *atom_w))
    x = transpose_mp(collect(got))
    return transpose_mp(atom_stage(x, atom_gain, atom_w)).reshape(A_DEV, F)


def solution(mesh):
    in_specs = (
        P("edge", "mp"),
        P("edge"),
        P("edge", None),
        P("edge", None),
        P("edge"),
        P(None, "mp"),
        P("mp", None),
        P(None, "mp"),
        P(None, "mp"),
        P(None, "mp"),
        P("mp", None),
        P(),
    )
    out_specs = P("edge", "mp")
    return jax.shard_map(body, mesh=mesh, in_specs=in_specs, out_specs=out_specs, check_vma=False)
```

```python
import jax
import jax.numpy as jnp
from jax import lax
from jax.experimental import pallas as pl
from jax.experimental.pallas import tpu as pltpu
from jax.sharding import PartitionSpec as P

A_DEV = 2048
GR = 32
AW = 16
MP = 4
F = 128
D = 512
ROWS = 2048
OWN = ROWS // MP
PIECE = OWN + 2 * D
GROUPS = ROWS // GR
OWNERS = 128
CAP = 2
HEAD = 8
VMEM = pltpu.VMEM
LIMIT = 24 * 1024 * 1024
ALL_VMEM = 63 * 1024 * 1024


def silu(v):
    return 0.5 * v * (1.0 + jnp.tanh(0.5 * v))


def vmem_spec():
    return pl.BlockSpec(memory_space=pltpu.VMEM)


def smem_spec():
    return pl.BlockSpec(memory_space=pltpu.SMEM)


def params():
    return pltpu.CompilerParams(vmem_limit_bytes=LIMIT)


def mm(a, b):
    return jnp.dot(a, b, preferred_element_type=jnp.float32)


def gather_kernel(rows_ref, mirror_ref, out_ref):
    half = ROWS // 2
    pick = jnp.concatenate(
        [jnp.broadcast_to(mirror_ref[j : j + 1, :], (F, F)).T for j in range(ROWS // F)], axis=0
    )
    within = pick & (half - 1)
    lanes = lax.broadcasted_iota(jnp.int32, (ROWS, F), 1)
    hot = jnp.concatenate(
        [jnp.where(within == lanes + j * F, 1.0, 0.0).astype(jnp.bfloat16) for j in range(half // F)], axis=1
    )
    got = mm(hot, jnp.concatenate([rows_ref[:half], rows_ref[half:]], axis=1))
    out_ref[...] = jnp.where(pick >= half, got[:, F:], got[:, :F]).astype(jnp.bfloat16)


def gather_rows(rows, mirror):
    return pl.pallas_call(
        gather_kernel,
        out_shape=jax.ShapeDtypeStruct((ROWS, F), jnp.bfloat16),
        in_specs=[vmem_spec()] * 2,
        out_specs=vmem_spec(),
        compiler_params=params(),
        cost_estimate=pl.CostEstimate(flops=20_000_000_000, bytes_accessed=64_000_000, transcendentals=0),
        name="gather_rows",
    )(rows, mirror.reshape(ROWS // F, F))


def windows_kernel(owner_ref, window_ref, out_ref):
    owner = owner_ref[...]
    hot = lax.broadcasted_iota(jnp.int32, (OWNERS, GROUPS), 0) == owner
    before = lax.broadcasted_iota(jnp.int32, (GROUPS, GROUPS), 0) < lax.broadcasted_iota(
        jnp.int32, (GROUPS, GROUPS), 1
    )
    rank = mm(
        jnp.where(hot, 1.0, 0.0).astype(jnp.bfloat16),
        jnp.where(before, 1.0, 0.0).astype(jnp.bfloat16),
    )
    value = window_ref[...].astype(jnp.float32) + 1.0
    lane = lax.broadcasted_iota(jnp.int32, (OWNERS, F), 1)
    out = jnp.full((OWNERS, F), -1.0, jnp.float32)
    for r in range(CAP):
        mine = jnp.where(hot & (rank == float(r)), value, 0.0)
        out = jnp.where(lane == r, jnp.sum(mine, axis=1, keepdims=True) - 1.0, out)
    out_ref[...] = out.astype(jnp.bfloat16)


def send_windows(owner, window):
    return pl.pallas_call(
        windows_kernel,
        out_shape=jax.ShapeDtypeStruct((OWNERS, F), jnp.bfloat16),
        in_specs=[vmem_spec()] * 2,
        out_specs=vmem_spec(),
        compiler_params=params(),
        name="send_windows",
    )(owner.reshape(1, GROUPS), window.reshape(1, GROUPS))


def after_kernel(slot_ref, rows_ref, out_ref):
    out_ref[...] = slot_ref[...]


def after_rows(slots, rows):
    return pl.pallas_call(
        after_kernel,
        out_shape=jax.ShapeDtypeStruct(slots.shape, slots.dtype),
        in_specs=[vmem_spec(), pl.BlockSpec(memory_space=pl.ANY)],
        out_specs=vmem_spec(),
        compiler_params=params(),
        cost_estimate=pl.CostEstimate(flops=40_000_000_000, bytes_accessed=128_000_000, transcendentals=0),
        name="after_rows",
    )(slots, rows)


def pack_kernel(*refs):
    *sources, out_ref, held, sems = refs
    copies = []
    for k, source in enumerate(sources):
        if source.shape[0] == D:
            moves = [(source, held.at[pl.ds(k * D, D)])]
        else:
            moves = [
                (source.at[:, pl.ds(j * F, F)], held.at[pl.ds(k * D + j * F, F)]) for j in range(MP)
            ]
        for source_part, part in moves:
            copies.append(pltpu.make_async_copy(source_part, part, sems.at[len(copies)]))
    for copy in copies:
        copy.start()
    for copy in copies:
        copy.wait()
    whole = pltpu.make_async_copy(held, out_ref, sems.at[len(copies)])
    whole.start()
    whole.wait()


def pack(*weights, limit):
    rows = len(weights) * D
    return pl.pallas_call(
        pack_kernel,
        out_shape=jax.ShapeDtypeStruct((rows, F), jnp.bfloat16),
        in_specs=[pl.BlockSpec(memory_space=pl.ANY)] * len(weights),
        out_specs=pl.BlockSpec(memory_space=pl.ANY),
        scratch_shapes=[pltpu.VMEM((rows, F), jnp.bfloat16), pltpu.SemaphoreType.DMA((len(weights) * MP + 1,))],
        compiler_params=pltpu.CompilerParams(vmem_limit_bytes=limit),
        name="pack_weights",
    )(*weights)


def core_index():
    return lax.rem(lax.axis_index("edge"), 2)


def share_kernel(rows_ref, up_ref, down_ref, self_ref, mirror_ref, out_ref, held, sems):
    def move(moves):
        copies = [pltpu.make_async_copy(src, dst, sems.at[k]) for k, (src, dst) in enumerate(moves)]
        for copy in copies:
            copy.start()
        for copy in copies:
            copy.wait()

    own = [(rows_ref, held.at[:, pl.ds(0, OWN)])]
    core = core_index()

    @pl.when(core == 0)
    def _():
        moves = list(own)
        for m in range(MP):
            moves.append((up_ref, held.at[m, pl.ds(OWN, D)]))
            for j in range(MP):
                moves.append((down_ref.at[:, pl.ds(j * F, F)], held.at[m, pl.ds(OWN + D + j * F, F)]))
        move(moves)

    @pl.when(core != 0)
    def _():
        moves = list(own)
        for m in range(MP):
            moves.append((self_ref, held.at[m, pl.ds(OWN, D)]))
            moves.append((mirror_ref, held.at[m, pl.ds(OWN + D, D)]))
        move(moves)

    move([(held, out_ref)])


def share(rows, *weights):
    return pl.pallas_call(
        share_kernel,
        out_shape=jax.ShapeDtypeStruct((MP, PIECE, F), jnp.bfloat16),
        in_specs=[pl.BlockSpec(memory_space=pl.ANY)] * 5,
        out_specs=pl.BlockSpec(memory_space=pl.ANY),
        scratch_shapes=[
            pltpu.VMEM((MP, PIECE, F), jnp.bfloat16),
            pltpu.SemaphoreType.DMA((1 + MP * (1 + MP),)),
        ],
        compiler_params=pltpu.CompilerParams(vmem_limit_bytes=ALL_VMEM),
        name="share_rows_and_weights",
    )(rows, *weights)


def wide(ref, start, pair):
    return jnp.concatenate(
        [ref[2 * pair, start : start + D, :], ref[2 * pair + 1, start : start + D, :]], axis=1
    )


def down_wide(ref, start, pair):
    blocks = [
        jnp.concatenate([ref[m, start + j * F : start + (j + 1) * F, :] for j in (2 * pair, 2 * pair + 1)], axis=1)
        for m in range(MP)
    ]
    return jnp.concatenate(blocks, axis=0)


def side_by_side(ref):
    return jnp.concatenate([ref[m] for m in range(MP)], axis=1)


def up(inputs, w_ref, at):
    return jnp.concatenate(
        [silu(mm(inputs, wide(w_ref, at, p))).astype(jnp.bfloat16) for p in range(2)], axis=1
    )


def down(hidden, base, w_ref, at):
    return [
        (base[:, 2 * F * p : 2 * F * (p + 1)].astype(jnp.float32) + mm(hidden, down_wide(w_ref, at, p))).astype(
            jnp.bfloat16
        )
        for p in range(2)
    ]


def edge_kernel(mine_ref, other_hbm, rev_ref, slot_ref, out_ref, other_ref, sems):
    copies = [
        pltpu.make_async_copy(
            other_hbm.at[:, pl.ds(OWN + k * D, D)], other_ref.at[:, pl.ds(OWN + k * D, D)], sems.at[k]
        )
        for k in range(2)
    ]
    for copy in copies:
        copy.start()

    def run(mlp_ref, mix_ref):
        own = jnp.concatenate([mine_ref[m, :OWN] for m in range(MP)], axis=1)
        rev = side_by_side(rev_ref)
        if mlp_ref is other_ref:
            copies[0].wait()
        own_hidden = up(own, mlp_ref, OWN)
        rev_hidden = up(rev, mlp_ref, OWN)
        if mlp_ref is other_ref:
            copies[1].wait()
        one = jnp.concatenate(down(own_hidden, own, mlp_ref, OWN + D), axis=1)
        reverse = jnp.concatenate(down(rev_hidden, rev, mlp_ref, OWN + D), axis=1)
        if mix_ref is other_ref:
            copies[0].wait()
            copies[1].wait()
        groups = OWN // GR
        at = lax.broadcasted_iota(jnp.int32, (groups * AW, OWN), 0)
        target = slot_ref[...] + (lax.broadcasted_iota(jnp.int32, (1, OWN), 1) // GR) * AW
        pick = jnp.where(at == target, 1.0, 0.0).astype(jnp.bfloat16)
        for p in range(2):
            mixed = mm(one, wide(mix_ref, OWN, p)) + mm(reverse, wide(mix_ref, OWN + D, p))
            two = (one[:, 2 * F * p : 2 * F * (p + 1)].astype(jnp.float32) + silu(mixed)).astype(jnp.bfloat16)
            sums = mm(pick, two).astype(jnp.bfloat16)
            out_ref[2 * p] = sums[:, :F]
            out_ref[2 * p + 1] = sums[:, F:]

    core = core_index()

    @pl.when(core == 0)
    def _():
        run(mine_ref, other_ref)

    @pl.when(core != 0)
    def _():
        run(other_ref, mine_ref)


def edge_stage(mine, other, rev, slots):
    return pl.pallas_call(
        edge_kernel,
        out_shape=jax.ShapeDtypeStruct((MP, OWN // GR * AW, F), jnp.bfloat16),
        in_specs=[vmem_spec(), pl.BlockSpec(memory_space=pl.ANY), vmem_spec(), vmem_spec()],
        out_specs=vmem_spec(),
        scratch_shapes=[pltpu.VMEM((MP, PIECE, F), jnp.bfloat16), pltpu.SemaphoreType.DMA((2,))],
        compiler_params=params(),
        name="edge_stage",
    )(mine, other, rev, slots)


def place_kernel(owner_ref, window_ref, blocks_ref, out_ref, seen_ref):
    @pl.loop(0, OWNERS, unroll=8)
    def _(o):
        seen_ref[o] = 0

    out_ref[:, : CAP * AW, :] = jnp.zeros((OWNERS, CAP * AW, F), jnp.bfloat16)
    out_ref[:, CAP * AW :, :] = jnp.full((OWNERS, HEAD, F), -1.0, jnp.bfloat16)
    line = lax.broadcasted_iota(jnp.int32, (HEAD, F), 0)

    @pl.loop(0, GROUPS, unroll=16)
    def _(g):
        owner = owner_ref[g]
        rank = seen_ref[owner]
        seen_ref[owner] = rank + 1
        out_ref[owner, pl.ds(pl.multiple_of(rank * AW, AW), AW), :] = blocks_ref[g]
        head = out_ref[owner, CAP * AW :, :].astype(jnp.float32)
        head = jnp.where(line == rank, window_ref[g].astype(jnp.float32), head)
        out_ref[owner, CAP * AW :, :] = head.astype(jnp.bfloat16)


def place(owner, window, blocks):
    return pl.pallas_call(
        place_kernel,
        out_shape=jax.ShapeDtypeStruct((OWNERS, CAP * AW + HEAD, F), jnp.bfloat16),
        in_specs=[smem_spec(), smem_spec(), vmem_spec()],
        out_specs=vmem_spec(),
        scratch_shapes=[pltpu.SMEM((OWNERS,), jnp.int32)],
        compiler_params=params(),
        name="place_groups",
    )(owner, window, blocks)


def collect_kernel(got_ref, out_ref, wide_ref, sum_ref):
    period = CAP * AW + HEAD
    wide_ref[...] = got_ref[...].astype(jnp.float32).reshape(OWNERS * period, F)
    lanes = lax.broadcasted_iota(jnp.int32, (OWNERS, F), 1).astype(jnp.float32)
    placing = jnp.concatenate(
        [
            jnp.where(wide_ref[pl.ds(CAP * AW + r, OWNERS, stride=period), :] == lanes, 1.0, 0.0).T
            for r in range(CAP)
        ],
        axis=1,
    ).astype(jnp.bfloat16)
    for a in range(0, AW, 2):
        rows = jnp.concatenate(
            [
                jnp.concatenate(
                    [wide_ref[pl.ds(r * AW + b, OWNERS, stride=period), :] for b in (a, a + 1)], axis=1
                )
                for r in range(CAP)
            ],
            axis=0,
        ).astype(jnp.bfloat16)
        sums = mm(placing, rows)
        sum_ref[pl.ds(a, A_DEV // AW, stride=AW), :] = sums[:, :F]
        sum_ref[pl.ds(a + 1, A_DEV // AW, stride=AW), :] = sums[:, F:]
    out_ref[...] = sum_ref[...].astype(jnp.bfloat16).reshape(MP, OWN, F)


def collect(got):
    return pl.pallas_call(
        collect_kernel,
        out_shape=jax.ShapeDtypeStruct((MP, OWN, F), jnp.bfloat16),
        in_specs=[vmem_spec()],
        out_specs=vmem_spec(),
        scratch_shapes=[
            pltpu.VMEM((OWNERS * (CAP * AW + HEAD), F), jnp.float32),
            pltpu.VMEM((A_DEV, F), jnp.float32),
        ],
        compiler_params=params(),
        name="collect_blocks",
    )(got)


def atom_kernel(x_ref, gain_ref, *refs):
    *shards, out_ref, w_ref = refs
    me = lax.axis_index("mp")
    for shift, shard in enumerate(shards):
        w_ref[lax.rem(me + MP - shift, MP)] = shard[...]
    base = side_by_side(x_ref)
    full = base.astype(jnp.float32)
    scale = lax.rsqrt(jnp.mean(full * full, axis=1, keepdims=True) + 1e-06)
    normed = (full * scale * gain_ref[...]).astype(jnp.bfloat16)
    out = down(up(normed, w_ref, 0), base, w_ref, D)
    for p in range(2):
        out_ref[2 * p] = out[p][:, :F]
        out_ref[2 * p + 1] = out[p][:, F:]


def atom_stage(x, gain, shards):
    return pl.pallas_call(
        atom_kernel,
        out_shape=jax.ShapeDtypeStruct((MP, OWN, F), jnp.bfloat16),
        in_specs=[vmem_spec()] * (2 + MP),
        out_specs=vmem_spec(),
        scratch_shapes=[pltpu.VMEM((MP, 2 * D, F), jnp.bfloat16)],
        compiler_params=params(),
        name="atom_stage",
    )(x, gain.reshape(1, D), *shards)


def transpose_mp(x):
    return lax.all_to_all(x, "mp", split_axis=0, concat_axis=0, tiled=True)


def body(
    edge_feat,
    mirror_rows,
    edge_slot,
    group_owner,
    group_window,
    up_edge,
    down_edge,
    mix_self,
    mix_mirror,
    up_atom,
    down_atom,
    atom_gain,
):
    half = OWNERS // 2
    partner = lax.ppermute(edge_feat, "edge", [(e, e ^ half) for e in range(OWNERS)])
    owner = group_owner.reshape(GROUPS)
    mine = transpose_mp(
        share(edge_feat.reshape(MP, OWN, F), up_edge, down_edge, mix_self, mix_mirror)
    )
    reverse, mine = lax.optimization_barrier((gather_rows(partner, mirror_rows), mine))
    rev = transpose_mp(reverse.reshape(MP, OWN, F))
    me = lax.axis_index("mp")
    slots = lax.dynamic_slice(edge_slot, (me * (OWN // F), 0), (OWN // F, F))
    slots, mine = lax.optimization_barrier((after_rows(slots, reverse), mine))
    other = lax.ppermute(mine, "edge", [(e, e ^ 1) for e in range(OWNERS)])
    partial = edge_stage(mine, other, rev, slots.reshape(1, OWN))
    blocks = transpose_mp(partial).reshape(GROUPS, AW, F)
    sent = place(owner, group_window, blocks)
    sent, up_atom, down_atom = lax.optimization_barrier((sent, up_atom, down_atom))
    atom_pack = pack(up_atom, down_atom, limit=LIMIT)
    atom_w = [atom_pack] + [
        lax.ppermute(atom_pack, "mp", [(m, (m + shift) % MP) for m in range(MP)]) for shift in range(1, MP)
    ]
    got = lax.all_to_all(sent, "edge", split_axis=0, concat_axis=0, tiled=True)
    got, *atom_w = lax.optimization_barrier((got, *atom_w))
    x = transpose_mp(collect(got))
    return transpose_mp(atom_stage(x, atom_gain, atom_w)).reshape(A_DEV, F)


def solution(mesh):
    in_specs = (
        P("edge", "mp"),
        P("edge"),
        P("edge", None),
        P("edge", None),
        P("edge"),
        P(None, "mp"),
        P("mp", None),
        P(None, "mp"),
        P(None, "mp"),
        P(None, "mp"),
        P("mp", None),
        P(),
    )
    out_specs = P("edge", "mp")
    return jax.shard_map(body, mesh=mesh, in_specs=in_specs, out_specs=out_specs, check_vma=False)
```

```python
import jax
import jax.numpy as jnp
from jax import lax
from jax.experimental import pallas as pl
from jax.experimental.pallas import tpu as pltpu
from jax.sharding import PartitionSpec as P

A_DEV = 2048
GR = 32
AW = 16
MP = 4
F = 128
D = 512
ROWS = 2048
OWN = ROWS // MP
PIECE = OWN + 2 * D
GROUPS = ROWS // GR
OWNERS = 128
CAP = 2
HEAD = 8
VMEM = pltpu.VMEM
LIMIT = 24 * 1024 * 1024
ALL_VMEM = 63 * 1024 * 1024


def silu(v):
    return 0.5 * v * (1.0 + jnp.tanh(0.5 * v))


def vmem_spec():
    return pl.BlockSpec(memory_space=pltpu.VMEM)


def smem_spec():
    return pl.BlockSpec(memory_space=pltpu.SMEM)


def params():
    return pltpu.CompilerParams(vmem_limit_bytes=LIMIT)


def mm(a, b):
    return jnp.dot(a, b, preferred_element_type=jnp.float32)


def gather_kernel(rows_ref, mirror_ref, out_ref):
    half = ROWS // 2
    pick = jnp.concatenate(
        [jnp.broadcast_to(mirror_ref[j : j + 1, :], (F, F)).T for j in range(ROWS // F)], axis=0
    )
    within = pick & (half - 1)
    lanes = lax.broadcasted_iota(jnp.int32, (ROWS, F), 1)
    hot = jnp.concatenate(
        [jnp.where(within == lanes + j * F, 1.0, 0.0).astype(jnp.bfloat16) for j in range(half // F)], axis=1
    )
    got = mm(hot, jnp.concatenate([rows_ref[:half], rows_ref[half:]], axis=1))
    out_ref[...] = jnp.where(pick >= half, got[:, F:], got[:, :F]).astype(jnp.bfloat16)


def gather_rows(rows, mirror):
    return pl.pallas_call(
        gather_kernel,
        out_shape=jax.ShapeDtypeStruct((ROWS, F), jnp.bfloat16),
        in_specs=[vmem_spec()] * 2,
        out_specs=vmem_spec(),
        compiler_params=params(),
        cost_estimate=pl.CostEstimate(flops=20_000_000_000, bytes_accessed=64_000_000, transcendentals=0),
        name="gather_rows",
    )(rows, mirror.reshape(ROWS // F, F))


def windows_kernel(owner_ref, window_ref, out_ref):
    owner = owner_ref[...]
    hot = lax.broadcasted_iota(jnp.int32, (OWNERS, GROUPS), 0) == owner
    before = lax.broadcasted_iota(jnp.int32, (GROUPS, GROUPS), 0) < lax.broadcasted_iota(
        jnp.int32, (GROUPS, GROUPS), 1
    )
    rank = mm(
        jnp.where(hot, 1.0, 0.0).astype(jnp.bfloat16),
        jnp.where(before, 1.0, 0.0).astype(jnp.bfloat16),
    )
    value = window_ref[...].astype(jnp.float32) + 1.0
    lane = lax.broadcasted_iota(jnp.int32, (OWNERS, F), 1)
    out = jnp.full((OWNERS, F), -1.0, jnp.float32)
    for r in range(CAP):
        mine = jnp.where(hot & (rank == float(r)), value, 0.0)
        out = jnp.where(lane == r, jnp.sum(mine, axis=1, keepdims=True) - 1.0, out)
    out_ref[...] = out.astype(jnp.bfloat16)


def send_windows(owner, window):
    return pl.pallas_call(
        windows_kernel,
        out_shape=jax.ShapeDtypeStruct((OWNERS, F), jnp.bfloat16),
        in_specs=[vmem_spec()] * 2,
        out_specs=vmem_spec(),
        compiler_params=params(),
        name="send_windows",
    )(owner.reshape(1, GROUPS), window.reshape(1, GROUPS))


def after_kernel(slot_ref, rows_ref, out_ref):
    out_ref[...] = slot_ref[...]


def after_rows(slots, rows):
    return pl.pallas_call(
        after_kernel,
        out_shape=jax.ShapeDtypeStruct(slots.shape, slots.dtype),
        in_specs=[vmem_spec(), pl.BlockSpec(memory_space=pl.ANY)],
        out_specs=vmem_spec(),
        compiler_params=params(),
        cost_estimate=pl.CostEstimate(flops=40_000_000_000, bytes_accessed=128_000_000, transcendentals=0),
        name="after_rows",
    )(slots, rows)


def pack_kernel(*refs):
    *sources, out_ref, held, sems = refs
    copies = []
    for k, source in enumerate(sources):
        if source.shape[0] == D:
            moves = [(source, held.at[pl.ds(k * D, D)])]
        else:
            moves = [
                (source.at[:, pl.ds(j * F, F)], held.at[pl.ds(k * D + j * F, F)]) for j in range(MP)
            ]
        for source_part, part in moves:
            copies.append(pltpu.make_async_copy(source_part, part, sems.at[len(copies)]))
    for copy in copies:
        copy.start()
    for copy in copies:
        copy.wait()
    whole = pltpu.make_async_copy(held, out_ref, sems.at[len(copies)])
    whole.start()
    whole.wait()


def pack(*weights, limit):
    rows = len(weights) * D
    return pl.pallas_call(
        pack_kernel,
        out_shape=jax.ShapeDtypeStruct((rows, F), jnp.bfloat16),
        in_specs=[pl.BlockSpec(memory_space=pl.ANY)] * len(weights),
        out_specs=pl.BlockSpec(memory_space=pl.ANY),
        scratch_shapes=[pltpu.VMEM((rows, F), jnp.bfloat16), pltpu.SemaphoreType.DMA((len(weights) * MP + 1,))],
        compiler_params=pltpu.CompilerParams(vmem_limit_bytes=limit),
        name="pack_weights",
    )(*weights)


def core_index():
    return lax.rem(lax.axis_index("edge"), 2)


def share_kernel(rows_ref, up_ref, down_ref, self_ref, mirror_ref, out_ref, held, weights, sems):
    def copies(moves, first):
        made = [pltpu.make_async_copy(src, dst, sems.at[first + k]) for k, (src, dst) in enumerate(moves)]
        for copy in made:
            copy.start()
        return made

    def wait(made):
        for copy in made:
            copy.wait()

    rows_in = copies([(rows_ref, held)], 0)
    core = core_index()

    @pl.when(core == 0)
    def _():
        moves = [(up_ref, weights.at[pl.ds(0, D)])]
        for j in range(MP):
            moves.append((down_ref.at[:, pl.ds(j * F, F)], weights.at[pl.ds(D + j * F, F)]))
        wait(copies(moves, 1))

    @pl.when(core != 0)
    def _():
        wait(copies([(self_ref, weights.at[pl.ds(0, D)]), (mirror_ref, weights.at[pl.ds(D, D)])], 1))

    out = copies([(weights, out_ref.at[m, pl.ds(OWN, 2 * D)]) for m in range(MP)], 2 + MP)
    wait(rows_in)
    out += copies([(held, out_ref.at[:, pl.ds(0, OWN)])], 2 + 2 * MP)
    wait(out)


def share(rows, *weights):
    return pl.pallas_call(
        share_kernel,
        out_shape=jax.ShapeDtypeStruct((MP, PIECE, F), jnp.bfloat16),
        in_specs=[pl.BlockSpec(memory_space=pl.ANY)] * 5,
        out_specs=pl.BlockSpec(memory_space=pl.ANY),
        scratch_shapes=[
            pltpu.VMEM((MP, OWN, F), jnp.bfloat16),
            pltpu.VMEM((2 * D, F), jnp.bfloat16),
            pltpu.SemaphoreType.DMA((3 + 2 * MP,)),
        ],
        compiler_params=pltpu.CompilerParams(vmem_limit_bytes=ALL_VMEM),
        name="share_rows_and_weights",
    )(rows, *weights)


def wide(ref, start, pair):
    return jnp.concatenate(
        [ref[2 * pair, start : start + D, :], ref[2 * pair + 1, start : start + D, :]], axis=1
    )


def down_wide(ref, start, pair):
    blocks = [
        jnp.concatenate([ref[m, start + j * F : start + (j + 1) * F, :] for j in (2 * pair, 2 * pair + 1)], axis=1)
        for m in range(MP)
    ]
    return jnp.concatenate(blocks, axis=0)


def side_by_side(ref):
    return jnp.concatenate([ref[m] for m in range(MP)], axis=1)


def up(inputs, w_ref, at):
    return jnp.concatenate(
        [silu(mm(inputs, wide(w_ref, at, p))).astype(jnp.bfloat16) for p in range(2)], axis=1
    )


def down(hidden, base, w_ref, at):
    return [
        (base[:, 2 * F * p : 2 * F * (p + 1)].astype(jnp.float32) + mm(hidden, down_wide(w_ref, at, p))).astype(
            jnp.bfloat16
        )
        for p in range(2)
    ]


def edge_kernel(mine_ref, other_hbm, rev_ref, slot_ref, out_ref, other_ref, sems):
    copies = [
        pltpu.make_async_copy(
            other_hbm.at[:, pl.ds(OWN + k * D, D)], other_ref.at[:, pl.ds(OWN + k * D, D)], sems.at[k]
        )
        for k in range(2)
    ]
    for copy in copies:
        copy.start()

    def run(mlp_ref, mix_ref):
        own = jnp.concatenate([mine_ref[m, :OWN] for m in range(MP)], axis=1)
        rev = side_by_side(rev_ref)
        if mlp_ref is other_ref:
            copies[0].wait()
        own_hidden = up(own, mlp_ref, OWN)
        rev_hidden = up(rev, mlp_ref, OWN)
        if mlp_ref is other_ref:
            copies[1].wait()
        one = jnp.concatenate(down(own_hidden, own, mlp_ref, OWN + D), axis=1)
        reverse = jnp.concatenate(down(rev_hidden, rev, mlp_ref, OWN + D), axis=1)
        if mix_ref is other_ref:
            copies[0].wait()
            copies[1].wait()
        groups = OWN // GR
        at = lax.broadcasted_iota(jnp.int32, (groups * AW, OWN), 0)
        target = slot_ref[...] + (lax.broadcasted_iota(jnp.int32, (1, OWN), 1) // GR) * AW
        pick = jnp.where(at == target, 1.0, 0.0).astype(jnp.bfloat16)
        for p in range(2):
            mixed = mm(one, wide(mix_ref, OWN, p)) + mm(reverse, wide(mix_ref, OWN + D, p))
            two = (one[:, 2 * F * p : 2 * F * (p + 1)].astype(jnp.float32) + silu(mixed)).astype(jnp.bfloat16)
            sums = mm(pick, two).astype(jnp.bfloat16)
            out_ref[2 * p] = sums[:, :F]
            out_ref[2 * p + 1] = sums[:, F:]

    core = core_index()

    @pl.when(core == 0)
    def _():
        run(mine_ref, other_ref)

    @pl.when(core != 0)
    def _():
        run(other_ref, mine_ref)


def edge_stage(mine, other, rev, slots):
    return pl.pallas_call(
        edge_kernel,
        out_shape=jax.ShapeDtypeStruct((MP, OWN // GR * AW, F), jnp.bfloat16),
        in_specs=[vmem_spec(), pl.BlockSpec(memory_space=pl.ANY), vmem_spec(), vmem_spec()],
        out_specs=vmem_spec(),
        scratch_shapes=[pltpu.VMEM((MP, PIECE, F), jnp.bfloat16), pltpu.SemaphoreType.DMA((2,))],
        compiler_params=params(),
        name="edge_stage",
    )(mine, other, rev, slots)


def place_kernel(owner_ref, window_ref, blocks_ref, out_ref, seen_ref):
    @pl.loop(0, OWNERS, unroll=8)
    def _(o):
        seen_ref[o] = 0

    out_ref[:, : CAP * AW, :] = jnp.zeros((OWNERS, CAP * AW, F), jnp.bfloat16)
    out_ref[:, CAP * AW :, :] = jnp.full((OWNERS, HEAD, F), -1.0, jnp.bfloat16)
    line = lax.broadcasted_iota(jnp.int32, (HEAD, F), 0)

    @pl.loop(0, GROUPS, unroll=16)
    def _(g):
        owner = owner_ref[g]
        rank = seen_ref[owner]
        seen_ref[owner] = rank + 1
        out_ref[owner, pl.ds(pl.multiple_of(rank * AW, AW), AW), :] = blocks_ref[g]
        head = out_ref[owner, CAP * AW :, :].astype(jnp.float32)
        head = jnp.where(line == rank, window_ref[g].astype(jnp.float32), head)
        out_ref[owner, CAP * AW :, :] = head.astype(jnp.bfloat16)


def place(owner, window, blocks):
    return pl.pallas_call(
        place_kernel,
        out_shape=jax.ShapeDtypeStruct((OWNERS, CAP * AW + HEAD, F), jnp.bfloat16),
        in_specs=[smem_spec(), smem_spec(), vmem_spec()],
        out_specs=vmem_spec(),
        scratch_shapes=[pltpu.SMEM((OWNERS,), jnp.int32)],
        compiler_params=params(),
        name="place_groups",
    )(owner, window, blocks)


def collect_kernel(got_ref, out_ref, wide_ref, sum_ref):
    period = CAP * AW + HEAD
    wide_ref[...] = got_ref[...].astype(jnp.float32).reshape(OWNERS * period, F)
    lanes = lax.broadcasted_iota(jnp.int32, (OWNERS, F), 1).astype(jnp.float32)
    placing = jnp.concatenate(
        [
            jnp.where(wide_ref[pl.ds(CAP * AW + r, OWNERS, stride=period), :] == lanes, 1.0, 0.0).T
            for r in range(CAP)
        ],
        axis=1,
    ).astype(jnp.bfloat16)
    for a in range(0, AW, 2):
        rows = jnp.concatenate(
            [
                jnp.concatenate(
                    [wide_ref[pl.ds(r * AW + b, OWNERS, stride=period), :] for b in (a, a + 1)], axis=1
                )
                for r in range(CAP)
            ],
            axis=0,
        ).astype(jnp.bfloat16)
        sums = mm(placing, rows)
        sum_ref[pl.ds(a, A_DEV // AW, stride=AW), :] = sums[:, :F]
        sum_ref[pl.ds(a + 1, A_DEV // AW, stride=AW), :] = sums[:, F:]
    out_ref[...] = sum_ref[...].astype(jnp.bfloat16).reshape(MP, OWN, F)


def collect(got):
    return pl.pallas_call(
        collect_kernel,
        out_shape=jax.ShapeDtypeStruct((MP, OWN, F), jnp.bfloat16),
        in_specs=[vmem_spec()],
        out_specs=vmem_spec(),
        scratch_shapes=[
            pltpu.VMEM((OWNERS * (CAP * AW + HEAD), F), jnp.float32),
            pltpu.VMEM((A_DEV, F), jnp.float32),
        ],
        compiler_params=params(),
        name="collect_blocks",
    )(got)


def atom_kernel(x_ref, gain_ref, *refs):
    *shards, out_ref, w_ref = refs
    me = lax.axis_index("mp")
    for shift, shard in enumerate(shards):
        w_ref[lax.rem(me + MP - shift, MP)] = shard[...]
    base = side_by_side(x_ref)
    full = base.astype(jnp.float32)
    scale = lax.rsqrt(jnp.mean(full * full, axis=1, keepdims=True) + 1e-06)
    normed = (full * scale * gain_ref[...]).astype(jnp.bfloat16)
    out = down(up(normed, w_ref, 0), base, w_ref, D)
    for p in range(2):
        out_ref[2 * p] = out[p][:, :F]
        out_ref[2 * p + 1] = out[p][:, F:]


def atom_stage(x, gain, shards):
    return pl.pallas_call(
        atom_kernel,
        out_shape=jax.ShapeDtypeStruct((MP, OWN, F), jnp.bfloat16),
        in_specs=[vmem_spec()] * (2 + MP),
        out_specs=vmem_spec(),
        scratch_shapes=[pltpu.VMEM((MP, 2 * D, F), jnp.bfloat16)],
        compiler_params=params(),
        name="atom_stage",
    )(x, gain.reshape(1, D), *shards)


def transpose_mp(x):
    return lax.all_to_all(x, "mp", split_axis=0, concat_axis=0, tiled=True)


def body(
    edge_feat,
    mirror_rows,
    edge_slot,
    group_owner,
    group_window,
    up_edge,
    down_edge,
    mix_self,
    mix_mirror,
    up_atom,
    down_atom,
    atom_gain,
):
    half = OWNERS // 2
    partner = lax.ppermute(edge_feat, "edge", [(e, e ^ half) for e in range(OWNERS)])
    owner = group_owner.reshape(GROUPS)
    mine = transpose_mp(
        share(edge_feat.reshape(MP, OWN, F), up_edge, down_edge, mix_self, mix_mirror)
    )
    reverse, mine = lax.optimization_barrier((gather_rows(partner, mirror_rows), mine))
    rev = transpose_mp(reverse.reshape(MP, OWN, F))
    me = lax.axis_index("mp")
    slots = lax.dynamic_slice(edge_slot, (me * (OWN // F), 0), (OWN // F, F))
    slots, mine = lax.optimization_barrier((after_rows(slots, reverse), mine))
    other = lax.ppermute(mine, "edge", [(e, e ^ 1) for e in range(OWNERS)])
    partial = edge_stage(mine, other, rev, slots.reshape(1, OWN))
    blocks = transpose_mp(partial).reshape(GROUPS, AW, F)
    sent = place(owner, group_window, blocks)
    sent, up_atom, down_atom = lax.optimization_barrier((sent, up_atom, down_atom))
    atom_pack = pack(up_atom, down_atom, limit=LIMIT)
    atom_w = [atom_pack] + [
        lax.ppermute(atom_pack, "mp", [(m, (m + shift) % MP) for m in range(MP)]) for shift in range(1, MP)
    ]
    got = lax.all_to_all(sent, "edge", split_axis=0, concat_axis=0, tiled=True)
    got, *atom_w = lax.optimization_barrier((got, *atom_w))
    x = transpose_mp(collect(got))
    return transpose_mp(atom_stage(x, atom_gain, atom_w)).reshape(A_DEV, F)


def solution(mesh):
    in_specs = (
        P("edge", "mp"),
        P("edge"),
        P("edge", None),
        P("edge", None),
        P("edge"),
        P(None, "mp"),
        P("mp", None),
        P(None, "mp"),
        P(None, "mp"),
        P(None, "mp"),
        P("mp", None),
        P(),
    )
    out_specs = P("edge", "mp")
    return jax.shard_map(body, mesh=mesh, in_specs=in_specs, out_specs=out_specs, check_vma=False)
```
